256 devices in a mesh: row: 16 (over y, x), col: 16 (over z, core).
Axes of the slice: x: 4, y: 4, z: 8, core: 2. Of those that a mesh axis runs over, the one named last changes fastest.
Arguments:
- inputs: bfloat16 [768, 8192], P('col', 'row'), may hold values from -6 to 6
- w_gate: bfloat16 [8192, 28672], P('row', 'col'), may hold values from -0.0625 to 0.0625
- w_up: bfloat16 [8192, 28672], P('row', 'col'), may hold values from -0.0625 to 0.0625
- w_down: bfloat16 [28672, 8192], P('col', 'row'), may hold values from -0.03125 to 0.03125
- cotangent: bfloat16 [768, 8192], P('col', 'row'), may hold values from -6 to 6
Outputs:
- output: bfloat16 [768, 8192], P('col', 'row')
- input_grad: bfloat16 [768, 8192], P('col', 'row')
- gate_grad: bfloat16 [8192, 28672], P('row', 'col')
- up_grad: bfloat16 [8192, 28672], P('row', 'col')
- down_grad: bfloat16 [28672, 8192], P('col', 'row')
The draws below stay inside these ranges and needn't reach their ends.
All inputs are finite; a program needn't handle non-finite values.
Results may differ from the reference program's by a relative error of at most 0.035.
Values may be sent and summed in bfloat16 or wider, within the bound.
A program may use at most 128 MiB of HBM per device.

```python
import jax
import jax.numpy as jnp
from jax import lax

D = 8192
FF = 28672
TOKENS = 768
N_ROW = 16
N_COL = 16


def steps_of(stream_key, dims, split, least, largest):
    loudness, own = 1.0, jax.random.fold_in(stream_key, 6)
    for position, shards_of in split:
        steps = jnp.exp(jax.random.uniform(jax.random.fold_in(own, position), (shards_of,), jnp.float32, least / len(split), largest / len(split)))
        loudness = loudness * jnp.repeat(steps, dims[position] // shards_of).reshape([-1 if axis == position else 1 for axis in range(len(dims))])
    return loudness


def scatter_about(key, shape, scale, most, cuts=(), kind=jnp.bfloat16):
    array = jax.random.normal(key, shape, jnp.float32) * scale
    if len(cuts) > 0:
        array = steps_of(key, shape, cuts, -0.22, 0.18) * array
    return jnp.clip(array, min=-most, max=most).astype(kind)


def setup_inputs(seed: int = 0) -> dict:
    arg_keys = jax.random.split(jax.random.key(seed), 6)
    inputs = scatter_about(arg_keys[0], (TOKENS, D), 1.0, 6.0, ((0, 16), (1, 16)))
    w_gate = scatter_about(arg_keys[1], (D, FF), D ** -0.5, 0.0625, ((0, 16), (1, 16)))
    w_up = scatter_about(arg_keys[2], (D, FF), D ** -0.5, 0.0625, ((0, 16), (1, 16)))
    w_down = scatter_about(arg_keys[3], (FF, D), FF ** -0.5, 0.03125, ((0, 16), (1, 16)))
    cotangent = scatter_about(arg_keys[4], (TOKENS, D), 1.0, 6.0, ((0, 16), (1, 16)))
    return {"inputs": inputs, "w_gate": w_gate, "w_up": w_up, "w_down": w_down, "cotangent": cotangent}


contract_rows = (((0,), (0,)), ((), ()))
contract_cols = (((1,), (1,)), ((), ()))


def round_term(value):
    rounded = lax.optimization_barrier(value.astype(jnp.bfloat16))
    return rounded.astype(jnp.float32)


def reference(inputs, w_gate, w_up, w_down, cotangent):
    width_block = D // N_ROW
    hidden_block = FF // N_COL
    gate = jnp.zeros((inputs.shape[0], FF), jnp.float32)
    up = jnp.zeros((inputs.shape[0], FF), jnp.float32)
    hidden_grad = jnp.zeros((inputs.shape[0], FF), jnp.float32)
    for block in range(N_ROW):
        lower = block * width_block
        upper = lower + width_block
        in_block = inputs[:, lower:upper]
        gate = gate + round_term(jnp.dot(in_block, w_gate[lower:upper], preferred_element_type=jnp.float32))
        up = up + round_term(jnp.dot(in_block, w_up[lower:upper], preferred_element_type=jnp.float32))
        hidden_grad = hidden_grad + round_term(lax.dot_general(cotangent[:, lower:upper], w_down[:, lower:upper], contract_cols, preferred_element_type=jnp.float32))
    sigmoid_gate = jax.nn.sigmoid(gate)
    hidden = (gate * sigmoid_gate * up).astype(jnp.bfloat16)
    down_grad = lax.dot_general(hidden, cotangent, contract_rows, preferred_element_type=jnp.float32).astype(jnp.bfloat16)
    gate_delta = (hidden_grad * up * sigmoid_gate * (1.0 + gate * (1.0 - sigmoid_gate))).astype(jnp.bfloat16)
    up_delta = (hidden_grad * gate * sigmoid_gate).astype(jnp.bfloat16)
    gate_grad = lax.dot_general(inputs, gate_delta, contract_rows, preferred_element_type=jnp.float32).astype(jnp.bfloat16)
    up_grad = lax.dot_general(inputs, up_delta, contract_rows, preferred_element_type=jnp.float32).astype(jnp.bfloat16)
    output_sum = jnp.zeros((inputs.shape[0], D), jnp.float32)
    input_sum = jnp.zeros((inputs.shape[0], D), jnp.float32)
    for block in range(N_COL):
        lower = block * hidden_block
        upper = lower + hidden_block
        output_sum = output_sum + round_term(jnp.dot(hidden[:, lower:upper], w_down[lower:upper], preferred_element_type=jnp.float32))
        first_term = lax.dot_general(gate_delta[:, lower:upper], w_gate[:, lower:upper], contract_cols, preferred_element_type=jnp.float32)
        second_term = lax.dot_general(up_delta[:, lower:upper], w_up[:, lower:upper], contract_cols, preferred_element_type=jnp.float32)
        input_sum = input_sum + round_term(first_term + second_term)
    output = output_sum.astype(jnp.bfloat16)
    input_grad = input_sum.astype(jnp.bfloat16)
    return (output, input_grad, gate_grad, up_grad, down_grad)
```

```python
import functools

import jax
import jax.numpy as jnp
from jax import lax
from jax.experimental import pallas as pl
from jax.experimental.pallas import tpu as pltpu
from jax.sharding import PartitionSpec as P

MESH = pl.DeviceIdType.MESH
ROWS = 16
CHUNKS = 3
BLOCKS = 16
CHIPS = 8
SETS = ((0, 512), (512, 512), (1024, 384), (1408, 384))
D, F = 512, 1792
WIDE = 896
BASE = (0, 8, 12, 14)

contract_rows = (((0,), (0,)), ((), ()))
contract_cols = (((1,), (1,)), ((), ()))


def place(stream, block):
    bits = [(block >> (3 - d)) & 1 for d in range(4)]
    index = 0
    for step in range(4):
        index = index * 2 + bits[(stream + step) % 4]
    return index


PLACES = [[place(j, k) for k in range(BLOCKS)] for j in range(4)]


def kernel(
    x_hbm, wg_hbm, wu_hbm, wd_hbm, ct_hbm,
    out_hbm, ig_hbm, gg_hbm, ug_hbm, dg_hbm,
    x_in, ct_in, xs, cts, wg, wu, wd,
    p_gu, r_gu, d_all, acc_g, acc_u, acc_d, gg, ug, dg, o_part, o_sib, o_z, o_fin,
    p_h0, p_h1, p_h2, p_h3, r_h0, r_h1, r_h2, r_h3, h0, h1, h2, h3,
    load_sem, store_sem, ssem, rsem, zs_sem, zr_sem,
):
    p_hg, r_hg, h_all = (p_h0, p_h1, p_h2, p_h3), (r_h0, r_h1, r_h2, r_h3), (h0, h1, h2, h3)
    row, col = lax.axis_index("row"), lax.axis_index("col")
    y, x = row // 4, row % 4
    z, core = col // 2, col % 2
    partner = (
        (y * 4 + x + 1 - 2 * (x % 2), col),
        ((y + 1 - 2 * (y % 2)) * 4 + x, col),
        (y * 4 + 3 - x, col),
        ((3 - y) * 4 + x, col),
    )
    bits = (((x + 1) // 2) % 2, ((y + 1) // 2) % 2, x // 2, y // 2)
    mine = []
    for j in range(4):
        index = 0
        for step in range(4):
            index = index * 2 + bits[(j + step) % 4]
        mine.append(index)
    sibling = (row, z * 2 + 1 - core)
    along = [(row, lax.rem(z + d, CHIPS) * 2 + core) for d in range(1, CHIPS)]

    loads = []
    for i, (src, dst) in enumerate(
        ((x_hbm, x_in), (ct_hbm, ct_in), (wg_hbm, wg), (wu_hbm, wu), (wd_hbm, wd))
    ):
        loads.append(pltpu.make_async_copy(src, dst, load_sem.at[i]))
        loads[-1].start()

    barrier = pltpu.get_barrier_semaphore()
    peers = list(partner) + along + [sibling]
    for peer in peers:
        pl.semaphore_signal(barrier, inc=1, device_id=peer, device_id_type=MESH)
    loads[0].wait()
    loads[1].wait()
    pl.semaphore_wait(barrier, len(peers))

    sent = []

    def send(src, dst, send_sem, recv_sem, device):
        copy = pltpu.make_async_remote_copy(
            src_ref=src, dst_ref=dst, send_sem=send_sem, recv_sem=recv_sem,
            device_id=device, device_id_type=MESH,
        )
        copy.start()
        sent.append(copy)
        return copy

    def gather_start(kind, c):
        buffer, own = ((xs, x_in), (cts, ct_in))[kind]
        block = own[c * ROWS:(c + 1) * ROWS, :]
        buffer[c, core, z] = block
        return [
            send(buffer.at[c, core, z], buffer.at[c, core, z], zs_sem.at[kind, c, d], zr_sem.at[kind, c, d], along[d])
            for d in range(CHIPS - 1)
        ]

    def gather_share(kind, c, copies):
        buffer = (xs, cts)[kind]
        for copy in copies:
            copy.wait_recv()
        return send(buffer.at[c, core], buffer.at[c, core], zs_sem.at[kind, c, 7], zr_sem.at[kind, c, 7], sibling)

    def rows_of(buffer, c):
        return buffer[c].reshape(BLOCKS * ROWS, D)

    def summed(lane, c, j):
        return (p_gu.at[c, j], r_gu.at[c, j]) if lane == 0 else (p_hg[j].at[c], r_hg[j].at[c])

    def gathered(lane, c, j):
        return h_all[j].at[c] if lane == 0 else d_all.at[c, j]

    flight = {}

    def reduce_send(lane, c, j, step):
        part, arrive = summed(lane, c, j)
        half = 8 >> step
        own = mine[j] // half * half
        other = own + half - 2 * half * (mine[j] // half % 2)
        flight[lane, c, j, step] = send(
            part.at[pl.ds(other, half)], arrive.at[pl.ds(BASE[step], half)],
            ssem.at[lane, c, j, step], rsem.at[lane, c, j, step], partner[(j + step) % 4],
        )

    def reduce_add(lane, c, j, step, first, count):
        part, arrive = summed(lane, c, j)
        half = 8 >> step
        own = mine[j] // half * half

        def body(i, carry):
            at = first + i
            part[at] = (
                part[at].astype(jnp.float32) + arrive[BASE[step] + at - own].astype(jnp.float32)
            ).astype(jnp.bfloat16)
            return carry

        lax.fori_loop(0, count, body, 0)

    def reduce_step(lane, c, j, step):
        flight[lane, c, j, step - 1].wait_recv()
        half = 8 >> step
        own = mine[j] // half * half
        other = own + half - 2 * half * (mine[j] // half % 2)
        reduce_add(lane, c, j, step - 1, other, half)
        reduce_send(lane, c, j, step)
        reduce_add(lane, c, j, step - 1, own, half)

    def reduce_last(lane, c, j):
        flight[lane, c, j, 3].wait_recv()
        part, arrive = summed(lane, c, j)
        return part[mine[j]].astype(jnp.float32) + arrive[BASE[3]].astype(jnp.float32)

    def gather_send(lane, c, j, step):
        buffer = gathered(lane, c, j)
        if step > 0:
            flight[lane, c, j, 3 + step].wait_recv()
        size = 1 << step
        region = buffer.at[pl.ds(mine[j] // size * size, size)]
        flight[lane, c, j, 4 + step] = send(
            region, region, ssem.at[lane, c, j, 4 + step], rsem.at[lane, c, j, 4 + step], partner[(j + 3 - step) % 4]
        )

    def store_partial(ref, j, lo, value):
        width = value.shape[1]
        value = value.astype(jnp.bfloat16)
        for k in range(BLOCKS):
            ref[PLACES[j][k], :, lo:lo + width] = value[k * ROWS:(k + 1) * ROWS, :]

    def gate_up(c, j):
        other = (j + 2) % 4
        value = rows_of(xs, c)
        lo, width = SETS[j]
        store_partial(p_gu.at[c, j], j, 0, jnp.dot(value, wg[:, lo:lo + width], preferred_element_type=jnp.float32))
        at = width
        lo, width = SETS[other]
        store_partial(p_gu.at[c, j], j, at, jnp.dot(value, wu[:, lo:lo + width], preferred_element_type=jnp.float32))

    def hidden_grad(c, j):
        lo, width = SETS[j]
        value = lax.dot_general(rows_of(cts, c), wd[lo:lo + width, :], contract_cols, preferred_element_type=jnp.float32)
        store_partial(p_hg[j].at[c], j, 0, value)

    kept = {}

    def make_hidden(c):
        sums = [reduce_last(0, c, j) for j in range(4)]
        for j in range(4):
            width = SETS[j][1]
            gate = sums[j][:, :width]
            up = sums[(j + 2) % 4][:, WIDE - width:]
            h_all[j][c, mine[j]] = (gate * jax.nn.sigmoid(gate) * up).astype(jnp.bfloat16)
            gather_send(0, c, j, 0)

    def make_deltas(c):
        sums = []
        for j in range(4):
            part, arrive = summed(0, c, j)
            sums.append(part[mine[j]].astype(jnp.float32) + arrive[BASE[3]].astype(jnp.float32))
        for j in range(4):
            other = (j + 2) % 4
            width = SETS[j][1]
            gate = sums[j][:, :width]
            up = sums[other][:, WIDE - width:]
            grad = reduce_last(1, c, j)
            s = jax.nn.sigmoid(gate)
            d_all[c, j, mine[j], :, :width] = (grad * up * s * (1.0 + gate * (1.0 - s))).astype(jnp.bfloat16)
            d_all[c, other, mine[other], :, WIDE - width:] = (grad * gate * s).astype(jnp.bfloat16)
        for j in range(4):
            gather_send(1, c, j, 0)

    def tokens(ref, c, j, lo, width):
        return jnp.concatenate([ref[c, PLACES[j][k], :, lo:lo + width] for k in range(BLOCKS)], axis=0)

    def hidden_of(c, j):
        return tokens(h_all[j], c, j, 0, SETS[j][1])

    def gate_delta_of(c, j):
        return tokens(d_all.at[:, j], c, j, 0, SETS[j][1])

    def up_delta_of(c, j):
        other = (j + 2) % 4
        return tokens(d_all.at[:, other], c, other, WIDE - SETS[j][1], SETS[j][1])

    def wait_gathered(lane, c):
        for j in range(4):
            flight[lane, c, j, 7].wait_recv()

    def scatter_start(kind, c, total):
        o_part[kind, c] = total.astype(jnp.bfloat16).reshape(2, CHIPS, ROWS, D)
        return send(o_part.at[kind, c, 1 - core], o_sib.at[kind, c], zs_sem.at[2 + kind, c, 7], zr_sem.at[2 + kind, c, 7], sibling)

    def scatter_along(kind, c, copy):
        copy.wait_recv()

        def body(i, carry):
            o_part[kind, c, core, i] = (
                o_part[kind, c, core, i].astype(jnp.float32) + o_sib[kind, c, i].astype(jnp.float32)
            ).astype(jnp.bfloat16)
            return carry

        lax.fori_loop(0, CHIPS, body, 0)
        return [
            send(
                o_part.at[kind, c, core, lax.rem(z + d + 1, CHIPS)], o_z.at[kind, c, d],
                zs_sem.at[2 + kind, c, d], zr_sem.at[2 + kind, c, d], along[d],
            )
            for d in range(CHIPS - 1)
        ]

    def scatter_end(kind, c, copies):
        for copy in copies:
            copy.wait_recv()
        total = o_part[kind, c, core, z].astype(jnp.float32)
        for d in range(CHIPS - 1):
            total = total + o_z[kind, c, d].astype(jnp.float32)
        o_fin[kind, c * ROWS:(c + 1) * ROWS, :] = total.astype(jnp.bfloat16)

    def output_part(c):
        total = None
        for j in range(4):
            lo, width = SETS[j]
            term = jnp.dot(hidden_of(c, j), wd[lo:lo + width, :], preferred_element_type=jnp.float32)
            total = term if total is None else total + term
        return scatter_start(0, c, total)

    def input_grad_part(c):
        total = None
        for j in range(4):
            lo, width = SETS[j]
            term = lax.dot_general(
                gate_delta_of(c, j), wg[:, lo:lo + width], contract_cols, preferred_element_type=jnp.float32
            ) + lax.dot_general(
                up_delta_of(c, j), wu[:, lo:lo + width], contract_cols, preferred_element_type=jnp.float32
            )
            total = term if total is None else total + term
        return scatter_start(1, c, total)

    def product(left, right, chunks):
        a = jnp.concatenate([left(c) for c in chunks], axis=0) if len(chunks) > 1 else left(chunks[0])
        b = jnp.concatenate([right(c) for c in chunks], axis=0) if len(chunks) > 1 else right(chunks[0])
        return lax.dot_general(a, b, contract_rows, preferred_element_type=jnp.float32)

    def down_grads(chunks, last):
        for j in range(4):
            lo, width = SETS[j]
            value = product(lambda c: hidden_of(c, j), lambda c: rows_of(cts, c), chunks)
            if last:
                dg[lo:lo + width, :] = (acc_d[lo:lo + width, :] + value).astype(jnp.bfloat16)
            else:
                acc_d[lo:lo + width, :] = value

    def input_side_grads(chunks, last):
        for j in range(4):
            lo, width = SETS[j]
            for acc, res, of in ((acc_g, gg, gate_delta_of), (acc_u, ug, up_delta_of)):
                value = product(lambda c: rows_of(xs, c), lambda c: of(c, j), chunks)
                if last:
                    res[:, lo:lo + width] = (acc[:, lo:lo + width] + value).astype(jnp.bfloat16)
                else:
                    acc[:, lo:lo + width] = value

    x_fly, ct_fly, share = {}, {}, {}
    x_fly[0] = gather_start(0, 0)
    ct_fly[0] = gather_start(1, 0)
    share[0, 0] = gather_share(0, 0, x_fly[0])
    loads[2].wait()
    loads[3].wait()
    share[0, 0].wait_recv()
    for j in range(4):
        gate_up(0, j)
        reduce_send(0, 0, j, 0)
    share[1, 0] = gather_share(1, 0, ct_fly[0])
    for c in (1, 2):
        x_fly[c] = gather_start(0, c)
        ct_fly[c] = gather_start(1, c)
    loads[4].wait()
    share[1, 0].wait_recv()
    for j in range(4):
        hidden_grad(0, j)
        reduce_send(1, 0, j, 0)

    def open_chunk(c):
        for j in range(4):
            reduce_send(0, c, j, 0)
        for j in range(4):
            reduce_send(1, c, j, 0)

    def prepare(c):
        share[0, c] = gather_share(0, c, x_fly[c])
        share[1, c] = gather_share(1, c, ct_fly[c])
        share[0, c].wait_recv()
        for j in range(4):
            gate_up(c, j)
        share[1, c].wait_recv()
        for j in range(4):
            hidden_grad(c, j)

    def advance(c, t):
        if t == 0:
            open_chunk(c)
        elif t < 4:
            for lane in (0, 1):
                for j in range(4):
                    reduce_step(lane, c, j, t)
        elif t == 4:
            make_hidden(c)
            make_deltas(c)
        else:
            for lane in (0, 1):
                for j in range(4):
                    gather_send(lane, c, j, t - 4)

    scatter = {}
    prepare(1)
    advance(0, 1)
    advance(0, 2)
    advance(1, 0)
    prepare(2)
    advance(0, 3)
    advance(1, 1)
    advance(0, 4)
    advance(1, 2)
    advance(2, 0)
    advance(0, 5)
    advance(1, 3)
    advance(2, 1)
    advance(1, 4)
    advance(2, 2)
    advance(0, 6)
    advance(2, 3)
    advance(1, 5)
    advance(0, 7)
    advance(2, 4)
    advance(1, 6)
    advance(2, 5)
    advance(1, 7)
    wait_gathered(0, 0)
    scatter[0, 0] = output_part(0)
    wait_gathered(1, 0)
    scatter[1, 0] = input_grad_part(0)
    advance(2, 6)
    wait_gathered(0, 1)
    scatter[0, 1] = output_part(1)
    wait_gathered(1, 1)
    scatter[1, 1] = input_grad_part(1)
    advance(2, 7)
    for c in (0, 1):
        for kind in (0, 1):
            scatter[kind, c] = scatter_along(kind, c, scatter[kind, c])
    down_grads((0, 1), False)
    input_side_grads((0, 1), False)
    wait_gathered(0, 2)
    scatter[0, 2] = output_part(2)
    down_grads((2,), True)
    stores = [pltpu.make_async_copy(dg, dg_hbm, store_sem.at[0])]
    stores[-1].start()
    scatter[0, 2] = scatter_along(0, 2, scatter[0, 2])
    for c in (0, 1):
        for kind in (0, 1):
            scatter_end(kind, c, scatter[kind, c])
    wait_gathered(1, 2)
    scatter[1, 2] = input_grad_part(2)
    scatter_end(0, 2, scatter[0, 2])
    scatter[1, 2] = scatter_along(1, 2, scatter[1, 2])
    input_side_grads((2,), True)
    for i, (src, dst) in enumerate(((gg, gg_hbm), (ug, ug_hbm), (o_fin.at[0], out_hbm))):
        stores.append(pltpu.make_async_copy(src, dst, store_sem.at[1 + i]))
        stores[-1].start()
    scatter_end(1, 2, scatter[1, 2])
    stores.append(pltpu.make_async_copy(o_fin.at[1], ig_hbm, store_sem.at[4]))
    stores[-1].start()
    for copy in sent:
        copy.wait_send()
    for copy in stores:
        copy.wait()


def local(inputs, w_gate, w_up, w_down, cotangent):
    bf16, f32 = jnp.bfloat16, jnp.float32
    vmem = pltpu.VMEM
    scratch = [
        vmem((CHUNKS * ROWS, D), bf16),
        vmem((CHUNKS * ROWS, D), bf16),
        vmem((CHUNKS, 2, CHIPS, ROWS, D), bf16),
        vmem((CHUNKS, 2, CHIPS, ROWS, D), bf16),
        vmem((D, F), bf16),
        vmem((D, F), bf16),
        vmem((F, D), bf16),
        vmem((CHUNKS, 4, BLOCKS, ROWS, WIDE), bf16),
        vmem((CHUNKS, 4, BLOCKS - 1, ROWS, WIDE), bf16),
        vmem((CHUNKS, 4, BLOCKS, ROWS, WIDE), bf16),
        vmem((D, F), f32),
        vmem((D, F), f32),
        vmem((F, D), f32),
        vmem((D, F), bf16),
        vmem((D, F), bf16),
        vmem((F, D), bf16),
        vmem((2, CHUNKS, 2, CHIPS, ROWS, D), bf16),
        vmem((2, CHUNKS, CHIPS, ROWS, D), bf16),
        vmem((2, CHUNKS, CHIPS - 1, ROWS, D), bf16),
        vmem((2, CHUNKS * ROWS, D), bf16),
    ]
    for count in (BLOCKS, BLOCKS - 1, BLOCKS):
        scratch += [vmem((CHUNKS, count, ROWS, width), bf16) for _, width in SETS]
    dma = pltpu.SemaphoreType.DMA
    scratch += [
        dma((5,)), dma((5,)),
        dma((2, CHUNKS, 4, 8)), dma((2, CHUNKS, 4, 8)),
        dma((4, CHUNKS, 8)), dma((4, CHUNKS, 8)),
    ]
    shape = jax.ShapeDtypeStruct
    return pl.pallas_call(
        kernel,
        out_shape=(
            shape(inputs.shape, bf16), shape(inputs.shape, bf16),
            shape(w_gate.shape, bf16), shape(w_up.shape, bf16), shape(w_down.shape, bf16),
        ),
        in_specs=[pl.BlockSpec(memory_space=pl.ANY)] * 5,
        out_specs=[pl.BlockSpec(memory_space=pl.ANY)] * 5,
        scratch_shapes=scratch,
        compiler_params=pltpu.CompilerParams(
            collective_id=0, has_side_effects=True, vmem_limit_bytes=62 * 2**20
        ),
    )(inputs, w_gate, w_up, w_down, cotangent)


def solution(mesh):
    return jax.shard_map(
        local,
        mesh=mesh,
        in_specs=(P("col", "row"), P("row", "col"), P("row", "col"), P("col", "row"), P("col", "row")),
        out_specs=(P("col", "row"), P("col", "row"), P("row", "col"), P("row", "col"), P("col", "row")),
        check_vma=False,
    )
```

```python
import jax
import jax.numpy as jnp
from jax import lax
from jax.experimental import pallas as pl
from jax.experimental.pallas import tpu as pltpu
from jax.sharding import PartitionSpec as P

MESH = pl.DeviceIdType.MESH
ROWS = 16
OWN = 48
CHUNKS = 3
BLOCKS = 16
CHIPS = 8
SETS = ((0, 512), (512, 512), (1024, 384), (1408, 384))
D, F = 512, 1792
WIDE = 896
HALF = 128
PARTS = 4
BASE = (0, 8, 12, 14)

SPOT = {1: 0, -1: 48, 0: 96, 2: 144, -2: 192, 4: 240, 3: 288, -3: 336}
FIRST = (0, 256, 128)
GROUPS = ((1, -1), (4, 3, -3), (2, -2))
SPANS = ((0, 96), (240, 144), (144, 96))
PARCELS = (
    ((1, 0, 48, 0), (-1, 48, 48, 0)),
    ((4, 0, 32, 16), (3, 32, 48, 0), (-3, 80, 48, 0)),
    ((4, 112, 16, 0), (2, 16, 48, 0), (-2, 64, 48, 0)),
)
LANDED = ((0, 96), (256, 128), (144, 112))

contract_rows = (((0,), (0,)), ((), ()))
contract_cols = (((1,), (1,)), ((), ()))

ORDER = (
    ("x", 0), ("c", 0), ("sx", 0), ("x", 1), ("x", 2), ("sc", 0), ("c", 2), ("c", 1), ("gu", 0, 2), ("gu", 0, 3),
    ("gu", 0, 1), ("hg", 0, 3), ("hg", 0, 0), ("hg", 0, 2), ("hg", 0, 1), ("gu", 0, 0), ("r", 1, 0, 2, 1), ("sx",
    1), ("r", 0, 0, 2, 1), ("r", 0, 0, 3, 1), ("r", 0, 0, 1, 1), ("sx", 2), ("gu", 1, 3), ("gu", 1, 1), ("gu", 1,
    0), ("gu", 2, 3), ("r", 1, 0, 3, 1), ("r", 1, 0, 1, 1), ("sc", 2), ("gu", 2, 2), ("r", 1, 0, 0, 1), ("r", 0, 0,
    0, 1), ("r", 1, 0, 2, 2), ("gu", 2, 0), ("gu", 1, 2), ("gu", 2, 1), ("r", 0, 0, 2, 2), ("r", 0, 0, 1, 2), ("r",
    0, 0, 3, 2), ("r", 1, 0, 3, 2), ("sc", 1), ("r", 0, 1, 1, 1), ("r", 0, 1, 3, 1), ("hg", 1, 3), ("hg", 1, 0),
    ("r", 0, 1, 0, 1), ("hg", 1, 1), ("hg", 1, 2), ("hg", 2, 0), ("r", 0, 0, 0, 2), ("r", 1, 0, 2, 3), ("hg", 2, 3),
    ("r", 1, 0, 1, 2), ("r", 0, 2, 2, 1), ("hg", 2, 2), ("hg", 2, 1), ("r", 0, 2, 3, 1), ("r", 1, 0, 0, 2), ("r", 0,
    2, 1, 1), ("r", 0, 1, 2, 1), ("r", 0, 2, 0, 1), ("r", 0, 0, 1, 3), ("r", 1, 0, 3, 3), ("r", 0, 0, 3, 3), ("r",
    0, 0, 2, 3), ("r", 0, 1, 1, 2), ("r", 1, 1, 3, 1), ("r", 0, 1, 3, 2), ("r", 1, 1, 1, 1), ("r", 1, 1, 0, 1),
    ("r", 0, 1, 0, 2), ("r", 1, 1, 2, 1), ("r", 0, 2, 2, 2), ("r", 1, 2, 3, 1), ("r", 1, 2, 2, 1), ("r", 1, 2, 0,
    1), ("r", 1, 0, 1, 3), ("r", 0, 0, 0, 3), ("r", 1, 2, 1, 1), ("r", 0, 2, 3, 2), ("r", 0, 2, 0, 2), ("r", 1, 0,
    0, 3), ("r", 0, 2, 1, 2), ("r", 0, 1, 2, 2), ("mh", 0, 1), ("r", 0, 1, 3, 3), ("r", 0, 1, 1, 3), ("r", 1, 1, 1,
    2), ("r", 1, 1, 3, 2), ("r", 1, 1, 2, 2), ("r", 1, 1, 0, 2), ("r", 0, 2, 2, 3), ("r", 0, 1, 0, 3), ("r", 1, 2,
    2, 2), ("r", 1, 2, 3, 2), ("r", 1, 2, 0, 2), ("r", 1, 2, 1, 2), ("md", 0, 1), ("r", 0, 2, 3, 3), ("mh", 0, 0),
    ("md", 0, 0), ("r", 1, 1, 1, 3), ("r", 0, 1, 2, 3), ("r", 0, 2, 0, 3), ("r", 0, 0, 1, 5), ("r", 0, 0, 3, 5),
    ("r", 0, 2, 1, 3), ("mh", 1, 1), ("r", 1, 1, 3, 3), ("r", 1, 1, 2, 3), ("r", 1, 1, 0, 3), ("r", 1, 2, 2, 3),
    ("r", 1, 2, 3, 3), ("r", 1, 2, 0, 3), ("r", 1, 2, 1, 3), ("r", 1, 0, 3, 5), ("r", 0, 0, 2, 5), ("r", 0, 0, 0,
    5), ("r", 1, 0, 1, 5), ("r", 1, 0, 2, 5), ("r", 1, 0, 0, 5), ("mh", 1, 0), ("mh", 2, 0), ("r", 0, 1, 3, 5),
    ("r", 0, 0, 3, 6), ("mh", 2, 1), ("r", 0, 1, 1, 5), ("r", 0, 0, 1, 6), ("md", 1, 1), ("md", 1, 0), ("md", 2, 0),
    ("md", 2, 1), ("r", 0, 0, 2, 6), ("r", 0, 0, 0, 6), ("r", 1, 0, 3, 6), ("r", 1, 0, 1, 6), ("r", 0, 1, 2, 5),
    ("r", 1, 0, 2, 6), ("r", 0, 1, 0, 5), ("r", 0, 2, 2, 5), ("r", 1, 0, 0, 6), ("r", 0, 2, 0, 5), ("r", 0, 2, 3,
    5), ("r", 0, 1, 3, 6), ("r", 0, 0, 3, 7), ("r", 0, 1, 1, 6), ("r", 1, 1, 2, 5), ("r", 0, 2, 1, 5), ("r", 1, 1,
    0, 5), ("r", 0, 0, 1, 7), ("r", 1, 2, 2, 5), ("r", 1, 1, 1, 5), ("r", 1, 2, 0, 5), ("r", 1, 1, 3, 5), ("r", 1,
    2, 1, 5), ("r", 1, 2, 3, 5), ("r", 0, 0, 0, 7), ("r", 0, 0, 2, 7), ("r", 1, 0, 3, 7), ("r", 1, 0, 1, 7), ("r",
    0, 1, 2, 6), ("r", 1, 0, 0, 7), ("r", 1, 0, 2, 7), ("r", 0, 2, 2, 6), ("r", 0, 1, 0, 6), ("r", 0, 2, 3, 6),
    ("r", 0, 2, 0, 6), ("r", 0, 1, 3, 7), ("r", 0, 1, 1, 7), ("r", 1, 1, 2, 6), ("r", 0, 2, 1, 6), ("r", 1, 1, 0,
    6), ("r", 1, 2, 2, 6), ("r", 1, 1, 1, 6), ("r", 1, 1, 3, 6), ("r", 1, 2, 0, 6), ("r", 1, 2, 1, 6), ("r", 1, 2,
    3, 6), ("m3", 0), ("al", 0, 0), ("r", 0, 1, 2, 7), ("m5", 0), ("r", 0, 2, 3, 7), ("r", 0, 2, 2, 7), ("r", 0, 1,
    0, 7), ("r", 0, 2, 1, 7), ("en", 0, 0), ("r", 0, 2, 0, 7), ("al", 1, 0), ("r", 1, 1, 3, 7), ("r", 1, 1, 1, 7),
    ("r", 1, 1, 2, 7), ("r", 1, 2, 3, 7), ("r", 1, 2, 1, 7), ("r", 1, 1, 0, 7), ("en", 1, 0), ("r", 1, 2, 2, 7),
    ("m3", 1), ("r", 1, 2, 0, 7), ("m4", 3), ("m4", 2), ("al", 0, 1), ("m4", 0), ("m3", 2), ("m4", 1), ("al", 0, 2),
    ("m5", 1), ("al", 1, 1), ("en", 0, 1), ("m6", 2), ("m5", 2), ("m6", 3), ("m6", 0), ("al", 1, 2), ("en", 0, 2),
    ("m6", 1), ("en", 1, 1), ("en", 1, 2),
)


def place(turn, block):
    bits = [(block >> (3 - d)) & 1 for d in range(4)]
    index = 0
    for step in range(4):
        index = index * 2 + bits[(turn + step) % 4]
    return index


PLACES = [[place(j, k) for k in range(BLOCKS)] for j in range(4)]


def kernel(
    x_hbm, wg_hbm, wu_hbm, wd_hbm, ct_hbm,
    out, ig, gg, ug, dg,
    x_in, ct_in, xs, cts, wg, wu, wd,
    p_gu, r_gu, d_all, o_part, o_sib, o_z, o_sum,
    p_h0, p_h1, p_h2, p_h3, r_h0, r_h1, r_h2, r_h3, h0, h1, h2, h3,
    load_sem, ssem, rsem, zs_sem, zr_sem, ss_sem, sr_sem,
):
    p_hg, r_hg, h_all = (p_h0, p_h1, p_h2, p_h3), (r_h0, r_h1, r_h2, r_h3), (h0, h1, h2, h3)
    row, col = lax.axis_index("row"), lax.axis_index("col")
    y, x = row // 4, row % 4
    z, core = col // 2, col % 2
    partner = (
        (y * 4 + x + 1 - 2 * (x % 2), col),
        ((y + 1 - 2 * (y % 2)) * 4 + x, col),
        (y * 4 + 3 - x, col),
        ((3 - y) * 4 + x, col),
    )
    bits = (((x + 1) // 2) % 2, ((y + 1) // 2) % 2, x // 2, y // 2)
    mine = []
    for turn in range(4):
        index = 0
        for step in range(4):
            index = index * 2 + bits[(turn + step) % 4]
        mine.append(index)
    sibling = (row, z * 2 + 1 - core)
    along = {d: (row, lax.rem(z + d + CHIPS, CHIPS) * 2 + core) for d in SPOT if d != 0}

    loads = []
    for i, (src, dst) in enumerate(
        ((x_hbm, x_in), (ct_hbm, ct_in), (wg_hbm, wg), (wu_hbm, wu), (wd_hbm, wd))
    ):
        loads.append(pltpu.make_async_copy(src, dst, load_sem.at[i]))
        loads[-1].start()

    barrier = pltpu.get_barrier_semaphore()
    peers = list(along.values()) + list(partner) + [sibling]
    for peer in peers:
        pl.semaphore_signal(barrier, inc=1, device_id=peer, device_id_type=MESH)
    loads[0].wait()
    loads[1].wait()
    pl.semaphore_wait(barrier, len(peers))

    def remote(src, dst, send_sem, recv_sem, device):
        return pltpu.make_async_remote_copy(
            src_ref=src, dst_ref=dst, send_sem=send_sem, recv_sem=recv_sem,
            device_id=device, device_id_type=MESH,
        )

    stores, sources = (xs, cts), (x_in, ct_in)
    first_done = set()

    def once(key, act):
        if key not in first_done:
            first_done.add(key)
            act()

    def span(kind, who, group):
        lo, count = SPANS[group]
        return stores[kind].at[who, pl.ds(lo, count)]

    def shared(kind, who, group):
        lo, count = SPANS[group]
        return stores[kind].at[who, pl.ds(lo, count + (OWN if group == 0 else 0))]

    def gather_start(kind, group):
        buffer, own = stores[kind], sources[kind]
        for d in GROUPS[group]:
            back = d if d == 4 else -d
            remote(
                own, buffer.at[core, pl.ds(SPOT[back], OWN)],
                zs_sem.at[kind, group], zr_sem.at[kind, group], along[d],
            ).start()
        if group == 0:
            spot = buffer.at[core, pl.ds(SPOT[0], OWN)]
            remote(own, spot, ss_sem.at[kind, 0], sr_sem.at[kind, 0], sibling).start()
            spot[...] = own[...]

    def gather_share(kind, group):
        whole = span(kind, core, group)
        remote(whole, whole, zs_sem.at[kind, group], zr_sem.at[kind, group], sibling).wait_recv()
        remote(whole, whole, ss_sem.at[kind, group], sr_sem.at[kind, group], sibling).start()

    def gather_end(kind, group):
        def act():
            whole = shared(kind, 1 - core, group)
            remote(whole, whole, ss_sem.at[kind, group], sr_sem.at[kind, group], sibling).wait_recv()
        once(("gathered", kind, group), act)

    def gather_sent(kind, group):
        whole, both = span(kind, core, group), shared(kind, core, group)
        remote(whole, whole, zs_sem.at[kind, group], zr_sem.at[kind, group], sibling).wait_send()
        remote(both, both, ss_sem.at[kind, group], sr_sem.at[kind, group], sibling).wait_send()

    def rows_of(buffer, c):
        return buffer[:, FIRST[c]:FIRST[c] + HALF, :].reshape(2 * HALF, D)

    def turn_of(lane, j, step):
        return (j + 2) % 4 if lane == 1 and step < 4 else j

    def dim_of(lane, j, step):
        turn = turn_of(lane, j, step)
        return (turn + step) % 4 if step < 4 else (turn + 7 - step) % 4

    def ends(lane, c, j, step):
        own = mine[turn_of(lane, j, step)]
        if step < 4:
            part, arrive = (p_gu.at[c, j], r_gu.at[c, j]) if lane == 0 else (p_hg[j].at[c], r_hg[j].at[c])
            half = 8 >> step
            keep = own // half * half
            give = keep + half - 2 * half * (own // half % 2)
            return part.at[pl.ds(give, half)], arrive.at[pl.ds(BASE[step], half)]
        buffer = h_all[j].at[c] if lane == 0 else d_all.at[c, j]
        size = 1 << (step - 4)
        region = buffer.at[pl.ds(own // size * size, size)]
        return region, region

    SLOT = (0, 1, 2, 3, 2, 1, 0, 4)

    def copy_of(lane, c, j, step):
        turn = turn_of(lane, j, step)
        src, dst = ends(lane, c, j, step)
        return remote(
            src, dst, ssem.at[lane, c, turn, step % 2], rsem.at[lane, c, turn, SLOT[step]],
            partner[dim_of(lane, j, step)],
        )

    def launch(lane, c, j, step):
        if step >= 2:
            before = j
            if turn_of(lane, j, step) != turn_of(lane, j, step - 2):
                before = (j + 2) % 4
            copy_of(lane, c, before, step - 2).wait_send()
        copy_of(lane, c, j, step).start()

    def arrived(lane, c, j, step):
        if step < 4:
            copy_of(lane, c, j, step).wait_recv()
        else:
            own = mine[j]
            size = 1 << (step - 4)
            buffer = h_all[j].at[c] if lane == 0 else d_all.at[c, j]
            keep = own // size * size
            other = buffer.at[pl.ds(keep + size - 2 * size * (own // size % 2), size)]
            remote(
                other, other, ssem.at[lane, c, j, step % 2], rsem.at[lane, c, j, SLOT[step]],
                partner[dim_of(lane, j, step)],
            ).wait_recv()

    def reduce_step(lane, c, j, step):
        arrived(lane, c, j, step - 1)
        part, arrive = (p_gu.at[c, j], r_gu.at[c, j]) if lane == 0 else (p_hg[j].at[c], r_hg[j].at[c])
        index = mine[turn_of(lane, j, step)]
        half, wide = 8 >> step, 16 >> step
        start = index // wide * wide
        keep = index // half * half
        give = keep + half - 2 * half * (index // half % 2)

        def add(first):
            def body(i, carry):
                at = first + i
                part[at] = (
                    part[at].astype(jnp.float32) + arrive[BASE[step - 1] + at - start].astype(jnp.float32)
                ).astype(jnp.bfloat16)
                return carry

            lax.fori_loop(0, half, body, 0)

        add(give)
        launch(lane, c, j, step)
        add(keep)

    def total_of(lane, c, j):
        part, arrive = (p_gu.at[c, j], r_gu.at[c, j]) if lane == 0 else (p_hg[j].at[c], r_hg[j].at[c])
        return part[mine[turn_of(lane, j, 0)]].astype(jnp.float32) + arrive[BASE[3]].astype(jnp.float32)

    def store_partial(ref, turn, lo, value):
        width = value.shape[1]
        value = value.astype(jnp.bfloat16)
        for k in range(BLOCKS):
            ref[PLACES[turn][k], :, lo:lo + width] = value[k * ROWS:(k + 1) * ROWS, :]

    def ready(kind, c):
        for group in ((0,), (1,), (1, 2))[c]:
            gather_end(kind, group)

    def gate_up(c, j):
        once("w_gate", loads[2].wait)
        once("w_up", loads[3].wait)
        ready(0, c)
        value = rows_of(xs, c)
        lo, width = SETS[j]
        store_partial(p_gu.at[c, j], j, 0, jnp.dot(value, wg[:, lo:lo + width], preferred_element_type=jnp.float32))
        at = width
        lo, width = SETS[(j + 2) % 4]
        store_partial(p_gu.at[c, j], j, at, jnp.dot(value, wu[:, lo:lo + width], preferred_element_type=jnp.float32))
        launch(0, c, j, 0)

    def hidden_grad(c, j):
        once("w_down", loads[4].wait)
        ready(1, c)
        lo, width = SETS[j]
        value = lax.dot_general(rows_of(cts, c), wd[lo:lo + width, :], contract_cols, preferred_element_type=jnp.float32)
        store_partial(p_hg[j].at[c], (j + 2) % 4, 0, value)
        launch(1, c, j, 0)

    def make_hidden(c, pair):
        streams = (pair, pair + 2)
        for j in streams:
            arrived(0, c, j, 3)
        sums = {j: total_of(0, c, j) for j in streams}
        for j in streams:
            width = SETS[j][1]
            gate = sums[j][:, :width]
            up = sums[(j + 2) % 4][:, WIDE - width:]
            h_all[j][c, mine[j]] = (gate * jax.nn.sigmoid(gate) * up).astype(jnp.bfloat16)
            launch(0, c, j, 4)

    def make_deltas(c, pair):
        streams = (pair, pair + 2)
        for j in streams:
            arrived(1, c, j, 3)
        sums = {j: total_of(0, c, j) for j in streams}
        for j in streams:
            other = (j + 2) % 4
            width = SETS[j][1]
            gate = sums[j][:, :width]
            up = sums[other][:, WIDE - width:]
            grad = total_of(1, c, j)
            s = jax.nn.sigmoid(gate)
            d_all[c, j, mine[j], :, :width] = (grad * up * s * (1.0 + gate * (1.0 - s))).astype(jnp.bfloat16)
            d_all[c, other, mine[other], :, WIDE - width:] = (grad * gate * s).astype(jnp.bfloat16)
        for j in streams:
            launch(1, c, j, 4)

    def tokens(ref, c, j, lo, width):
        return jnp.concatenate([ref[c, PLACES[j][k], :, lo:lo + width] for k in range(BLOCKS)], axis=0)

    def hidden_of(c, j):
        return tokens(h_all[j], c, j, 0, SETS[j][1])

    def gate_delta_of(c, j):
        return tokens(d_all.at[:, j], c, j, 0, SETS[j][1])

    def up_delta_of(c, j):
        other = (j + 2) % 4
        return tokens(d_all.at[:, other], c, other, WIDE - SETS[j][1], SETS[j][1])

    def gathered(lane, c, j):
        once(("doubled", lane, c, j), lambda: arrived(lane, c, j, 7))

    def scatter_start(kind, c, total):
        o_part[kind, c] = total.astype(jnp.bfloat16).reshape(2, HALF, D)
        once(("sent", kind, c), lambda: gather_sent(kind, c))
        remote(
            o_part.at[kind, c, 1 - core], o_sib.at[kind, c], ss_sem.at[kind, c], sr_sem.at[2 + kind, c], sibling
        ).start()

    def scatter_along(kind, c):
        remote(
            o_part.at[kind, c, 1 - core], o_sib.at[kind, c], ss_sem.at[kind, c], sr_sem.at[2 + kind, c], sibling
        ).wait_recv()
        o_part[kind, c, core] = (
            o_part[kind, c, core].astype(jnp.float32) + o_sib[kind, c].astype(jnp.float32)
        ).astype(jnp.bfloat16)
        for d, lo, count, at in PARCELS[c]:
            back = d if d == 4 else -d
            remote(
                o_part.at[kind, c, core, pl.ds(lo, count)], o_z.at[kind, pl.ds(SPOT[back] + at, count)],
                zs_sem.at[kind, c], zr_sem.at[2 + kind, c], along[d],
            ).start()

    def landed(kind, c):
        lo, count = LANDED[c]
        whole = o_z.at[kind, pl.ds(lo, count)]
        return remote(whole, whole, zs_sem.at[kind, c], zr_sem.at[2 + kind, c], sibling)

    def scatter_end(kind, c):
        landed(kind, c).wait_recv()
        f32 = jnp.float32

        def own(lo, count):
            return o_part[kind, c, core, lo:lo + count, :].astype(f32)

        def come(d, at, count):
            return o_z[kind, SPOT[d] + at:SPOT[d] + at + count, :].astype(f32)

        if c == 0:
            o_sum[kind] = come(1, 0, OWN) + come(-1, 0, OWN)
            o_sum[kind, 0:32, :] += own(96, 32)
        elif c == 1:
            o_sum[kind] += come(3, 0, OWN) + come(-3, 0, OWN)
            o_sum[kind, 16:48, :] += come(4, 16, 32)
        else:
            o_sum[kind, 0:16, :] += come(4, 0, 16)
            o_sum[kind, 32:48, :] += own(0, 16)
            (out, ig)[kind][...] = (o_sum[kind] + come(2, 0, OWN) + come(-2, 0, OWN)).astype(jnp.bfloat16)

    def output_part(c):
        total = None
        for j in range(4):
            gathered(0, c, j)
            lo, width = SETS[j]
            term = jnp.dot(hidden_of(c, j), wd[lo:lo + width, :], preferred_element_type=jnp.float32)
            total = term if total is None else total + term
        scatter_start(0, c, total)

    def input_grad_part(c):
        for j in range(4):
            gathered(1, c, j)
        total = None
        for j in range(4):
            lo, width = SETS[j]
            term = lax.dot_general(
                gate_delta_of(c, j), wg[:, lo:lo + width], contract_cols, preferred_element_type=jnp.float32
            ) + lax.dot_general(
                up_delta_of(c, j), wu[:, lo:lo + width], contract_cols, preferred_element_type=jnp.float32
            )
            total = term if total is None else total + term
        scatter_start(1, c, total)

    def over_tokens(left, right):
        a = jnp.concatenate([left(c) for c in range(CHUNKS)], axis=0)
        b = jnp.concatenate([right(c) for c in range(CHUNKS)], axis=0)
        return lax.dot_general(a, b, contract_rows, preferred_element_type=jnp.float32).astype(jnp.bfloat16)

    def down_grad(j):
        for c in range(CHUNKS):
            gathered(0, c, j)
        lo, width = SETS[j]
        dg[lo:lo + width, :] = over_tokens(lambda c: hidden_of(c, j), lambda c: rows_of(cts, c))

    def input_side_grads(j):
        for c in range(CHUNKS):
            gathered(1, c, j)
            gathered(1, c, (j + 2) % 4)
        lo, width = SETS[j]
        for res, of in ((gg, gate_delta_of), (ug, up_delta_of)):
            res[:, lo:lo + width] = over_tokens(lambda c: rows_of(xs, c), lambda c: of(c, j))

    def halve_or_double(lane, c, j, step):
        if step < 4:
            reduce_step(lane, c, j, step)
        else:
            arrived(lane, c, j, step - 1)
            launch(lane, c, j, step)

    acts = {
        "x": lambda c: gather_start(0, c), "c": lambda c: gather_start(1, c),
        "sx": lambda c: gather_share(0, c), "sc": lambda c: gather_share(1, c),
        "gu": gate_up, "hg": hidden_grad, "r": halve_or_double, "mh": make_hidden, "md": make_deltas,
        "m3": output_part, "m5": input_grad_part, "al": scatter_along, "en": scatter_end,
        "m4": down_grad, "m6": input_side_grads,
    }
    for act, *where in ORDER:
        acts[act](*where)

    for lane in range(2):
        for c in range(CHUNKS):
            for j in range(4):
                for step in (6, 7):
                    copy_of(lane, c, j, step).wait_send()
    for kind in range(2):
        for c in range(CHUNKS):
            landed(kind, c).wait_send()
            remote(
                o_part.at[kind, c, 1 - core], o_sib.at[kind, c], ss_sem.at[kind, c], sr_sem.at[2 + kind, c], sibling
            ).wait_send()


def deliver(*refs):
    sources, results, sem = refs[:5], refs[5:10], refs[10]
    copies = []
    for src, dst in zip(sources, results):
        parts = 1 if src.shape[0] == OWN else PARTS
        step = src.shape[0] // parts
        for lo in range(0, src.shape[0], step):
            rows = pl.ds(lo, step)
            copies.append(pltpu.make_async_copy(src.at[rows], dst.at[rows], sem.at[len(copies)]))
    for copy in copies:
        copy.start()
    for copy in copies:
        copy.wait()


def local(inputs, w_gate, w_up, w_down, cotangent):
    bf16, f32 = jnp.bfloat16, jnp.float32
    vmem = pltpu.VMEM
    scratch = [
        vmem((OWN, D), bf16),
        vmem((OWN, D), bf16),
        vmem((2, CHUNKS * HALF, D), bf16),
        vmem((2, CHUNKS * HALF, D), bf16),
        vmem((D, F), bf16),
        vmem((D, F), bf16),
        vmem((F, D), bf16),
        vmem((CHUNKS, 4, BLOCKS, ROWS, WIDE), bf16),
        vmem((CHUNKS, 4, BLOCKS - 1, ROWS, WIDE), bf16),
        vmem((CHUNKS, 4, BLOCKS, ROWS, WIDE), bf16),
        vmem((2, CHUNKS, 2, HALF, D), bf16),
        vmem((2, CHUNKS, HALF, D), bf16),
        vmem((2, CHUNKS * HALF, D), bf16),
        vmem((2, OWN, D), f32),
    ]
    for count in (BLOCKS, BLOCKS - 1, BLOCKS):
        scratch += [vmem((CHUNKS, count, ROWS, width), bf16) for _, width in SETS]
    dma = pltpu.SemaphoreType.DMA
    scratch += [
        dma((5,)), dma((2, CHUNKS, 4, 2)), dma((2, CHUNKS, 4, 5)),
        dma((2, CHUNKS)), dma((4, CHUNKS)), dma((2, CHUNKS)), dma((4, CHUNKS)),
    ]
    whole = pl.BlockSpec(memory_space=pltpu.HBM)
    here = pl.BlockSpec(memory_space=pltpu.VMEM)
    results = (inputs, inputs, w_gate, w_up, w_down)
    held = pl.pallas_call(
        kernel,
        out_shape=tuple(pltpu.VMEM(a.shape, bf16) for a in results),
        in_specs=[whole] * 5,
        out_specs=[here] * 5,
        scratch_shapes=scratch,
        compiler_params=pltpu.CompilerParams(
            collective_id=0, has_side_effects=True, vmem_limit_bytes=40 * 2**20
        ),
    )(*[pltpu.with_memory_space_constraint(a, pltpu.HBM) for a in (inputs, w_gate, w_up, w_down, cotangent)])
    held = [pltpu.with_memory_space_constraint(a, pltpu.VMEM) for a in held]
    return pl.pallas_call(
        deliver,
        out_shape=tuple(jax.ShapeDtypeStruct(a.shape, bf16) for a in results),
        in_specs=[here] * 5,
        out_specs=[whole] * 5,
        scratch_shapes=[dma((2 + 3 * PARTS,))],
        compiler_params=pltpu.CompilerParams(vmem_limit_bytes=2**20),
    )(*held)


def solution(mesh):
    return jax.shard_map(
        local,
        mesh=mesh,
        in_specs=(P("col", "row"), P("row", "col"), P("row", "col"), P("col", "row"), P("col", "row")),
        out_specs=(P("col", "row"), P("col", "row"), P("row", "col"), P("row", "col"), P("col", "row")),
        check_vma=False,
    )
```

```python
import jax
import jax.numpy as jnp
from jax import lax
from jax.experimental import pallas as pl
from jax.experimental.pallas import tpu as pltpu
from jax.sharding import PartitionSpec as P

MESH = pl.DeviceIdType.MESH
ROWS = 16
OWN = 48
CHUNKS = 3
BLOCKS = 16
CHIPS = 8
SETS = ((0, 512), (512, 512), (1024, 384), (1408, 384))
D, F = 512, 1792
WIDE = 896
HALF = 128
PARTS = 4
BASE = (0, 8, 12, 14)

SPOT = {0: 0, 1: 48, -1: 96, 2: 144, -2: 192, 3: 240, 4: 288, -3: 336}
FIRST = (0, 256, 128)
GROUPS = ((1, -1), (4, 3, -3), (2, -2))
SPANS = ((48, 96), (240, 144), (144, 96))
PARCELS = (
    ((1, 48, 48, 0), (-1, 96, 32, 0)),
    ((4, 32, 48, 0), (3, 0, 32, 16), (-3, 80, 48, 0)),
    ((3, 112, 16, 0), (2, 16, 48, 0), (-2, 64, 48, 0), (-1, 0, 16, 32)),
)
LANDED = (80, 128, 128)

contract_rows = (((0,), (0,)), ((), ()))
contract_cols = (((1,), (1,)), ((), ()))

ORDER = (
    ("c", 0), ("x", 0), ("sc", 0), ("c", 1), ("c", 2), ("hg", 0, 1), ("hg", 0, 2), ("sx", 0), ("hg", 0, 3), ("x",
    2), ("hg", 0, 0), ("x", 1), ("gu", 0, 1), ("gu", 0, 2), ("gu", 0, 0), ("gu", 0, 3), ("r", 1, 0, 2, 1), ("k", 1,
    0, 2, 1), ("r", 1, 0, 3, 1), ("r", 1, 0, 1, 1), ("k", 1, 0, 1, 1), ("k", 1, 0, 3, 1), ("r", 1, 0, 0, 1), ("k",
    1, 0, 0, 1), ("sc", 1), ("hg", 1, 0), ("hg", 1, 1), ("sc", 2), ("hg", 1, 2), ("hg", 1, 3), ("r", 0, 0, 0, 1),
    ("r", 0, 0, 1, 1), ("k", 0, 0, 1, 1), ("hg", 2, 2), ("r", 0, 0, 3, 1), ("k", 0, 0, 3, 1), ("k", 0, 0, 0, 1),
    ("hg", 2, 0), ("sx", 2), ("r", 0, 0, 2, 1), ("r", 1, 0, 1, 2), ("k", 0, 0, 2, 1), ("r", 1, 0, 2, 2), ("k", 1, 0,
    1, 2), ("hg", 2, 3), ("r", 1, 0, 0, 2), ("k", 1, 0, 0, 2), ("k", 1, 0, 2, 2), ("hg", 2, 1), ("r", 1, 0, 3, 2),
    ("k", 1, 0, 3, 2), ("r", 1, 1, 2, 1), ("k", 1, 1, 2, 1), ("r", 1, 1, 0, 1), ("k", 1, 1, 0, 1), ("r", 1, 1, 3,
    1), ("k", 1, 1, 3, 1), ("r", 1, 1, 1, 1), ("k", 1, 1, 1, 1), ("r", 1, 2, 2, 1), ("k", 1, 2, 2, 1), ("sx", 1),
    ("r", 0, 0, 1, 2), ("k", 0, 0, 1, 2), ("r", 0, 0, 0, 2), ("r", 0, 0, 2, 2), ("k", 0, 0, 2, 2), ("k", 0, 0, 0,
    2), ("gu", 1, 1), ("gu", 1, 3), ("gu", 1, 2), ("gu", 1, 0), ("r", 1, 0, 1, 3), ("r", 0, 0, 3, 2), ("k", 0, 0, 3,
    2), ("gu", 2, 2), ("r", 1, 0, 0, 3), ("r", 1, 2, 3, 1), ("k", 1, 2, 3, 1), ("r", 1, 2, 0, 1), ("k", 1, 2, 0, 1),
    ("k", 1, 0, 0, 3), ("r", 1, 2, 1, 1), ("k", 1, 2, 1, 1), ("gu", 2, 3), ("r", 1, 0, 2, 3), ("r", 1, 0, 3, 3),
    ("k", 1, 0, 2, 3), ("k", 1, 0, 3, 3), ("k", 1, 0, 1, 3), ("gu", 2, 0), ("r", 1, 1, 1, 2), ("k", 1, 1, 1, 2),
    ("gu", 2, 1), ("r", 1, 1, 3, 2), ("k", 1, 1, 3, 2), ("r", 1, 1, 2, 2), ("k", 1, 1, 2, 2), ("r", 1, 1, 0, 2),
    ("k", 1, 1, 0, 2), ("r", 1, 2, 2, 2), ("k", 1, 2, 2, 2), ("r", 0, 0, 2, 3), ("k", 0, 0, 2, 3), ("r", 0, 0, 0,
    3), ("k", 0, 0, 0, 3), ("r", 0, 0, 1, 3), ("k", 0, 0, 1, 3), ("r", 0, 1, 1, 1), ("k", 0, 1, 1, 1), ("r", 0, 1,
    0, 1), ("k", 0, 1, 0, 1), ("r", 0, 1, 2, 1), ("k", 0, 1, 2, 1), ("r", 0, 1, 3, 1), ("k", 0, 1, 3, 1), ("r", 0,
    0, 3, 3), ("k", 0, 0, 3, 3), ("r", 1, 2, 1, 2), ("k", 1, 2, 1, 2), ("r", 1, 1, 1, 3), ("k", 1, 1, 1, 3), ("r",
    1, 2, 0, 2), ("k", 1, 2, 0, 2), ("r", 0, 2, 2, 1), ("k", 0, 2, 2, 1), ("r", 1, 2, 3, 2), ("k", 1, 2, 3, 2),
    ("r", 0, 2, 0, 1), ("k", 0, 2, 0, 1), ("r", 0, 2, 1, 1), ("k", 0, 2, 1, 1), ("r", 0, 2, 3, 1), ("r", 1, 1, 2,
    3), ("k", 0, 2, 3, 1), ("k", 1, 1, 2, 3), ("r", 1, 1, 0, 3), ("k", 1, 1, 0, 3), ("r", 1, 2, 2, 3), ("k", 1, 2,
    2, 3), ("r", 1, 1, 3, 3), ("k", 1, 1, 3, 3), ("mh", 0, 0), ("md", 0, 0), ("r", 0, 1, 0, 2), ("k", 0, 1, 0, 2),
    ("r", 0, 1, 1, 2), ("k", 0, 1, 1, 2), ("r", 0, 1, 3, 2), ("k", 0, 1, 3, 2), ("r", 1, 2, 1, 3), ("k", 1, 2, 1,
    3), ("mh", 0, 1), ("r", 0, 1, 2, 2), ("md", 0, 1), ("k", 0, 1, 2, 2), ("r", 1, 2, 0, 3), ("k", 1, 2, 0, 3),
    ("r", 0, 2, 0, 2), ("k", 0, 2, 0, 2), ("r", 0, 2, 2, 2), ("k", 0, 2, 2, 2), ("r", 0, 2, 1, 2), ("r", 0, 2, 3,
    2), ("k", 0, 2, 1, 2), ("k", 0, 2, 3, 2), ("r", 0, 0, 2, 5), ("r", 1, 2, 3, 3), ("k", 1, 2, 3, 3), ("r", 0, 0,
    1, 5), ("r", 1, 0, 2, 5), ("r", 0, 1, 0, 3), ("r", 0, 0, 0, 5), ("k", 0, 1, 0, 3), ("r", 0, 0, 3, 5), ("r", 1,
    0, 0, 5), ("r", 0, 1, 2, 3), ("r", 0, 1, 3, 3), ("k", 0, 1, 3, 3), ("k", 0, 1, 2, 3), ("r", 1, 0, 3, 5), ("r",
    1, 0, 1, 5), ("r", 0, 1, 1, 3), ("k", 0, 1, 1, 3), ("r", 0, 2, 0, 3), ("k", 0, 2, 0, 3), ("r", 0, 2, 2, 3),
    ("k", 0, 2, 2, 3), ("r", 0, 2, 3, 3), ("k", 0, 2, 3, 3), ("r", 0, 2, 1, 3), ("k", 0, 2, 1, 3), ("r", 0, 0, 2,
    6), ("r", 0, 0, 0, 6), ("r", 0, 0, 1, 6), ("r", 0, 0, 3, 6), ("mh", 1, 0), ("md", 1, 0), ("r", 1, 0, 0, 6),
    ("r", 1, 0, 2, 6), ("mh", 1, 1), ("md", 1, 1), ("r", 1, 0, 1, 6), ("r", 1, 0, 3, 6), ("mh", 2, 0), ("md", 2, 0),
    ("mh", 2, 1), ("md", 2, 1), ("r", 0, 0, 2, 7), ("r", 0, 0, 0, 7), ("r", 0, 0, 3, 7), ("r", 0, 0, 1, 7), ("r", 0,
    1, 0, 5), ("r", 0, 1, 2, 5), ("r", 1, 1, 0, 5), ("r", 1, 1, 2, 5), ("r", 0, 1, 3, 5), ("r", 0, 1, 1, 5), ("r",
    1, 1, 3, 5), ("r", 1, 1, 1, 5), ("r", 1, 0, 2, 7), ("r", 1, 0, 0, 7), ("r", 0, 2, 2, 5), ("r", 0, 2, 0, 5),
    ("r", 1, 0, 1, 7), ("r", 1, 0, 3, 7), ("r", 1, 2, 2, 5), ("r", 1, 2, 0, 5), ("r", 0, 2, 3, 5), ("r", 0, 2, 1,
    5), ("r", 1, 2, 3, 5), ("r", 1, 2, 1, 5), ("r", 0, 1, 1, 6), ("r", 0, 1, 3, 6), ("r", 0, 1, 0, 6), ("m3", 0),
    ("r", 0, 1, 2, 6), ("r", 1, 1, 1, 6), ("r", 1, 1, 3, 6), ("r", 1, 1, 0, 6), ("al", 0, 0), ("r", 1, 1, 2, 6),
    ("en", 0, 0), ("r", 0, 2, 1, 6), ("r", 0, 2, 3, 6), ("r", 0, 2, 0, 6), ("m5", 0), ("r", 1, 2, 0, 6), ("r", 1, 2,
    3, 6), ("r", 0, 2, 2, 6), ("r", 1, 2, 1, 6), ("r", 0, 1, 2, 7), ("r", 1, 2, 2, 6), ("al", 1, 0), ("r", 0, 1, 0,
    7), ("r", 0, 1, 1, 7), ("r", 0, 1, 3, 7), ("r", 1, 1, 2, 7), ("r", 1, 1, 0, 7), ("r", 1, 1, 1, 7), ("r", 1, 1,
    3, 7), ("r", 0, 2, 2, 7), ("r", 0, 2, 0, 7), ("en", 1, 0), ("r", 0, 2, 3, 7), ("r", 0, 2, 1, 7), ("r", 1, 2, 2,
    7), ("r", 1, 2, 0, 7), ("r", 1, 2, 3, 7), ("r", 1, 2, 1, 7), ("m3", 1), ("al", 0, 1), ("m5", 1), ("al", 1, 1),
    ("m3", 2), ("m4", 0), ("m4", 3), ("al", 0, 2), ("m4", 1), ("m4", 2), ("en", 0, 1), ("m5", 2), ("m6", 2), ("al",
    1, 2), ("m6", 3), ("m6", 1), ("en", 1, 1), ("m6", 0), ("en", 0, 2), ("en", 1, 2),
)


def place(turn, block):
    bits = [(block >> (3 - d)) & 1 for d in range(4)]
    index = 0
    for step in range(4):
        index = index * 2 + bits[(turn + step) % 4]
    return index


PLACES = [[place(j, k) for k in range(BLOCKS)] for j in range(4)]


def kernel(
    x_hbm, wg_hbm, wu_hbm, wd_hbm, ct_hbm,
    out, ig, gg, ug, dg,
    x_in, ct_in, xs, cts, wg, wu, wd,
    p_gu, r_gu, d_all, o_part, o_sib, o_z, o_sum,
    p_h0, p_h1, p_h2, p_h3, r_h0, r_h1, r_h2, r_h3, h0, h1, h2, h3,
    load_sem, ssem, rsem, last_sem, zs_sem, zr_sem, ss_sem, sr_sem,
):
    p_hg, r_hg, h_all = (p_h0, p_h1, p_h2, p_h3), (r_h0, r_h1, r_h2, r_h3), (h0, h1, h2, h3)
    row, col = lax.axis_index("row"), lax.axis_index("col")
    y, x = row // 4, row % 4
    z, core = col // 2, col % 2
    partner = (
        (y * 4 + x + 1 - 2 * (x % 2), col),
        ((y + 1 - 2 * (y % 2)) * 4 + x, col),
        (y * 4 + 3 - x, col),
        ((3 - y) * 4 + x, col),
    )
    bits = (((x + 1) // 2) % 2, ((y + 1) // 2) % 2, x // 2, y // 2)
    mine = []
    for turn in range(4):
        index = 0
        for step in range(4):
            index = index * 2 + bits[(turn + step) % 4]
        mine.append(index)
    sibling = (row, z * 2 + 1 - core)
    along = {d: (row, lax.rem(z + d * (1 - 2 * core) + CHIPS, CHIPS) * 2 + core) for d in SPOT if d != 0}

    loads = []
    for i, (src, dst) in enumerate(
        ((x_hbm, x_in), (ct_hbm, ct_in), (wg_hbm, wg), (wu_hbm, wu), (wd_hbm, wd))
    ):
        loads.append(pltpu.make_async_copy(src, dst, load_sem.at[i]))
        loads[-1].start()

    barrier = pltpu.get_barrier_semaphore()
    peers = list(along.values()) + list(partner) + [sibling]
    for peer in peers:
        pl.semaphore_signal(barrier, inc=1, device_id=peer, device_id_type=MESH)
    loads[0].wait()
    loads[1].wait()
    pl.semaphore_wait(barrier, len(peers))

    def remote(src, dst, send_sem, recv_sem, device):
        return pltpu.make_async_remote_copy(
            src_ref=src, dst_ref=dst, send_sem=send_sem, recv_sem=recv_sem,
            device_id=device, device_id_type=MESH,
        )

    stores, sources = (xs, cts), (x_in, ct_in)
    first_done = set()

    def once(key, act):
        if key not in first_done:
            first_done.add(key)
            act()

    def span(kind, who, group):
        lo, count = SPANS[group]
        return stores[kind].at[who, pl.ds(lo, count)]

    def shared(kind, who, group):
        lo, count = SPANS[group]
        extra = OWN if group == 0 else 0
        return stores[kind].at[who, pl.ds(lo - extra, count + extra)]

    def gather_start(kind, group):
        buffer, own = stores[kind], sources[kind]
        for d in GROUPS[group]:
            back = d if d == 4 else -d
            remote(
                own, buffer.at[core, pl.ds(SPOT[back], OWN)],
                zs_sem.at[kind, group], zr_sem.at[kind, group], along[d],
            ).start()
        if group == 0:
            spot = buffer.at[core, pl.ds(SPOT[0], OWN)]
            remote(own, spot, ss_sem.at[kind, 0], sr_sem.at[kind, 0], sibling).start()
            spot[...] = own[...]

    def gather_share(kind, group):
        whole = span(kind, core, group)
        remote(whole, whole, zs_sem.at[kind, group], zr_sem.at[kind, group], sibling).wait_recv()
        remote(whole, whole, ss_sem.at[kind, group], sr_sem.at[kind, group], sibling).start()

    def gather_end(kind, group):
        def act():
            whole = shared(kind, 1 - core, group)
            remote(whole, whole, ss_sem.at[kind, group], sr_sem.at[kind, group], sibling).wait_recv()
        once(("gathered", kind, group), act)

    def gather_sent(kind, group):
        whole, both = span(kind, core, group), shared(kind, core, group)
        remote(whole, whole, zs_sem.at[kind, group], zr_sem.at[kind, group], sibling).wait_send()
        remote(both, both, ss_sem.at[kind, group], sr_sem.at[kind, group], sibling).wait_send()

    def rows_of(buffer, c):
        return buffer[:, FIRST[c]:FIRST[c] + HALF, :].reshape(2 * HALF, D)

    def turn_of(lane, j, step):
        return (j + 2) % 4 if lane == 1 and step < 4 else j

    def dim_of(lane, j, step):
        turn = turn_of(lane, j, step)
        return (turn + step) % 4 if step < 4 else (turn + 7 - step) % 4

    def ends(lane, c, j, step):
        own = mine[turn_of(lane, j, step)]
        if step < 4:
            part, arrive = (p_gu.at[c, j], r_gu.at[c, j]) if lane == 0 else (p_hg[j].at[c], r_hg[j].at[c])
            half = 8 >> step
            keep = own // half * half
            give = keep + half - 2 * half * (own // half % 2)
            return part.at[pl.ds(give, half)], arrive.at[pl.ds(BASE[step], half)]
        buffer = h_all[j].at[c] if lane == 0 else d_all.at[c, j]
        size = 1 << (step - 4)
        region = buffer.at[pl.ds(own // size * size, size)]
        return region, region

    SLOT = (0, 1, 2, 3, 2, 1, 0)

    def semaphores(lane, c, j, step):
        if lane == 0:
            leaving = ssem.at[0] if step < 4 else ssem.at[1 + j]
        else:
            leaving = ssem.at[5 + j] if step < 4 else ssem.at[9]
        coming = last_sem.at[lane, c] if step == 7 else rsem.at[lane, c, turn_of(lane, j, step), SLOT[step]]
        return leaving, coming

    def copy_of(lane, c, j, step):
        return remote(
            *ends(lane, c, j, step), *semaphores(lane, c, j, step), partner[dim_of(lane, j, step)]
        )

    def launch(lane, c, j, step):
        copy_of(lane, c, j, step).start()

    def arrived(lane, c, j, step):
        if step < 4:
            copy_of(lane, c, j, step).wait_recv()
        else:
            own = mine[j]
            size = 1 << (step - 4)
            buffer = h_all[j].at[c] if lane == 0 else d_all.at[c, j]
            keep = own // size * size
            other = buffer.at[pl.ds(keep + size - 2 * size * (own // size % 2), size)]
            remote(
                other, other, *semaphores(lane, c, j, step), partner[dim_of(lane, j, step)]
            ).wait_recv()

    def add_arrived(lane, c, j, step, given):
        part, arrive = (p_gu.at[c, j], r_gu.at[c, j]) if lane == 0 else (p_hg[j].at[c], r_hg[j].at[c])
        index = mine[turn_of(lane, j, step)]
        half, wide = 8 >> step, 16 >> step
        start = index // wide * wide
        keep = index // half * half
        give = keep + half - 2 * half * (index // half % 2)

        first = give if given else keep

        def body(i, carry):
            at = first + i
            part[at] = (
                part[at].astype(jnp.float32) + arrive[BASE[step - 1] + at - start].astype(jnp.float32)
            ).astype(jnp.bfloat16)
            return carry

        lax.fori_loop(0, half, body, 0)

    def reduce_step(lane, c, j, step):
        arrived(lane, c, j, step - 1)
        add_arrived(lane, c, j, step, True)
        launch(lane, c, j, step)

    def reduce_rest(lane, c, j, step):
        add_arrived(lane, c, j, step, False)

    def total_of(lane, c, j):
        part, arrive = (p_gu.at[c, j], r_gu.at[c, j]) if lane == 0 else (p_hg[j].at[c], r_hg[j].at[c])
        return part[mine[turn_of(lane, j, 0)]].astype(jnp.float32) + arrive[BASE[3]].astype(jnp.float32)

    def store_partial(ref, turn, lo, value):
        width = value.shape[1]
        value = value.astype(jnp.bfloat16)
        for k in range(BLOCKS):
            ref[PLACES[turn][k], :, lo:lo + width] = value[k * ROWS:(k + 1) * ROWS, :]

    def ready(kind, c):
        for group in ((0,), (1,), (0, 1, 2))[c]:
            gather_end(kind, group)

    def gate_up(c, j):
        once("w_gate", loads[2].wait)
        once("w_up", loads[3].wait)
        ready(0, c)
        value = rows_of(xs, c)
        lo, width = SETS[j]
        store_partial(p_gu.at[c, j], j, 0, jnp.dot(value, wg[:, lo:lo + width], preferred_element_type=jnp.float32))
        at = width
        lo, width = SETS[(j + 2) % 4]
        store_partial(p_gu.at[c, j], j, at, jnp.dot(value, wu[:, lo:lo + width], preferred_element_type=jnp.float32))
        launch(0, c, j, 0)

    def hidden_grad(c, j):
        once("w_down", loads[4].wait)
        ready(1, c)
        lo, width = SETS[j]
        value = lax.dot_general(rows_of(cts, c), wd[lo:lo + width, :], contract_cols, preferred_element_type=jnp.float32)
        store_partial(p_hg[j].at[c], (j + 2) % 4, 0, value)
        launch(1, c, j, 0)

    def make_hidden(c, pair):
        streams = (pair, pair + 2)
        for j in streams:
            arrived(0, c, j, 3)
        sums = {j: total_of(0, c, j) for j in streams}
        for j in streams:
            width = SETS[j][1]
            gate = sums[j][:, :width]
            up = sums[(j + 2) % 4][:, WIDE - width:]
            h_all[j][c, mine[j]] = (gate * jax.nn.sigmoid(gate) * up).astype(jnp.bfloat16)
            launch(0, c, j, 4)

    def make_deltas(c, pair):
        streams = (pair, pair + 2)
        for j in streams:
            arrived(1, c, j, 3)
        sums = {j: total_of(0, c, j) for j in streams}
        for j in streams:
            other = (j + 2) % 4
            width = SETS[j][1]
            gate = sums[j][:, :width]
            up = sums[other][:, WIDE - width:]
            grad = total_of(1, c, j)
            s = jax.nn.sigmoid(gate)
            d_all[c, j, mine[j], :, :width] = (grad * up * s * (1.0 + gate * (1.0 - s))).astype(jnp.bfloat16)
            d_all[c, other, mine[other], :, WIDE - width:] = (grad * gate * s).astype(jnp.bfloat16)
        for j in streams:
            launch(1, c, j, 4)

    def tokens(ref, c, j, lo, width, half=None):
        if half is None:
            places = PLACES[j]
        else:
            places = [place + half * (8 >> (4 - j) % 4) for place in PLACES[j][:BLOCKS // 2]]
        return jnp.concatenate([ref[c, place, :, lo:lo + width] for place in places], axis=0)

    def hidden_of(c, j):
        return tokens(h_all[j], c, j, 0, SETS[j][1])

    def gate_delta_of(c, j, half=None):
        return tokens(d_all.at[:, j], c, j, 0, SETS[j][1], half)

    def up_delta_of(c, j, half=None):
        other = (j + 2) % 4
        return tokens(d_all.at[:, other], c, other, WIDE - SETS[j][1], SETS[j][1], half)

    def gathered(lane, c):
        def act():
            size = p_gu.at[c, 0] if lane == 0 else d_all.at[c, :, pl.ds(0, 8)]
            remote(size, size, ssem.at[1], last_sem.at[lane, c], sibling).wait_recv()
        once(("doubled", lane, c), act)

    def scatter_start(kind, c, total):
        o_part[kind, c] = total.astype(jnp.bfloat16).reshape(2, HALF, D)
        scatter_share(kind, c)

    def scatter_share(kind, c):
        once(("sent", kind, c), lambda: gather_sent(kind, c))
        remote(
            o_part.at[kind, c, 1 - core], o_sib.at[kind, c], ss_sem.at[kind, c], sr_sem.at[2 + kind, c], sibling
        ).start()

    def scatter_along(kind, c):
        remote(
            o_part.at[kind, c, 1 - core], o_sib.at[kind, c], ss_sem.at[kind, c], sr_sem.at[2 + kind, c], sibling
        ).wait_recv()
        o_part[kind, c, core] = (
            o_part[kind, c, core].astype(jnp.float32) + o_sib[kind, c].astype(jnp.float32)
        ).astype(jnp.bfloat16)
        for d, lo, count, at in PARCELS[c]:
            back = d if d == 4 else -d
            remote(
                o_part.at[kind, c, core, pl.ds(lo, count)], o_z.at[kind, pl.ds(SPOT[back] + at, count)],
                zs_sem.at[kind, c], zr_sem.at[2 + kind, c], along[d],
            ).start()

    def landed(kind, c):
        whole = o_z.at[kind, pl.ds(0, LANDED[c])]
        return remote(whole, whole, zs_sem.at[kind, c], zr_sem.at[2 + kind, c], sibling)

    def scatter_end(kind, c):
        landed(kind, c).wait_recv()
        f32 = jnp.float32

        def own(lo, count):
            return o_part[kind, c, core, lo:lo + count, :].astype(f32)

        def come(d, at, count):
            return o_z[kind, SPOT[d] + at:SPOT[d] + at + count, :].astype(f32)

        if c == 0:
            o_sum[kind] = own(0, OWN) + come(-1, 0, OWN)
            o_sum[kind, 0:32, :] += come(1, 0, 32)
        elif c == 1:
            o_sum[kind] += come(3, 0, OWN) + come(4, 0, OWN)
            o_sum[kind, 16:48, :] += come(-3, 16, 32)
        else:
            o_sum[kind, 0:16, :] += come(-3, 0, 16)
            o_sum[kind, 32:48, :] += come(1, 32, 16)
            (out, ig)[kind][...] = (o_sum[kind] + come(2, 0, OWN) + come(-2, 0, OWN)).astype(jnp.bfloat16)

    def output_part(c):
        gathered(0, c)
        total = None
        for j in range(4):
            lo, width = SETS[j]
            term = jnp.dot(hidden_of(c, j), wd[lo:lo + width, :], preferred_element_type=jnp.float32)
            total = term if total is None else total + term
        scatter_start(0, c, total)

    def input_grad_part(c):
        gathered(1, c)

        def product(half):
            total = None
            for j in range(4):
                lo, width = SETS[j]
                term = lax.dot_general(
                    gate_delta_of(c, j, half), wg[:, lo:lo + width], contract_cols, preferred_element_type=jnp.float32
                ) + lax.dot_general(
                    up_delta_of(c, j, half), wu[:, lo:lo + width], contract_cols, preferred_element_type=jnp.float32
                )
                total = term if total is None else total + term
            return total

        if c < CHUNKS - 1:
            scatter_start(1, c, product(None))
        else:
            o_part[1, c, 1 - core] = product(1 - core).astype(jnp.bfloat16)
            scatter_share(1, c)
            o_part[1, c, core] = product(core).astype(jnp.bfloat16)

    def over_tokens(left, right):
        a = jnp.concatenate([left(c) for c in range(CHUNKS)], axis=0)
        b = jnp.concatenate([right(c) for c in range(CHUNKS)], axis=0)
        return lax.dot_general(a, b, contract_rows, preferred_element_type=jnp.float32).astype(jnp.bfloat16)

    def down_grad(j):
        for c in range(CHUNKS):
            gathered(0, c)
        lo, width = SETS[j]
        dg[lo:lo + width, :] = over_tokens(lambda c: hidden_of(c, j), lambda c: rows_of(cts, c))

    def input_side_grads(j):
        for c in range(CHUNKS):
            gathered(1, c)
        lo, width = SETS[j]
        for res, of in ((gg, gate_delta_of), (ug, up_delta_of)):
            res[:, lo:lo + width] = over_tokens(lambda c: rows_of(xs, c), lambda c: of(c, j))

    def halve_or_double(lane, c, j, step):
        if step < 4:
            reduce_step(lane, c, j, step)
        else:
            arrived(lane, c, j, step - 1)
            launch(lane, c, j, step)

    acts = {
        "x": lambda c: gather_start(0, c), "c": lambda c: gather_start(1, c),
        "sx": lambda c: gather_share(0, c), "sc": lambda c: gather_share(1, c),
        "gu": gate_up, "hg": hidden_grad, "r": halve_or_double, "k": reduce_rest, "mh": make_hidden, "md": make_deltas,
        "m3": output_part, "m5": input_grad_part, "al": scatter_along, "en": scatter_end,
        "m4": down_grad, "m6": input_side_grads,
    }
    for act, *where in ORDER:
        acts[act](*where)

    left = [(r_gu, 0)]
    for j in range(4):
        left += [(h_all[j].at[:, pl.ds(0, BLOCKS - 1)], 1 + j), (r_hg[j], 5 + j)]
    left.append((d_all.at[:, :, pl.ds(0, BLOCKS - 1)], 9))
    for size, i in left:
        remote(size, size, ssem.at[i], last_sem.at[0, 0], sibling).wait_send()
    for kind in range(2):
        for c in range(CHUNKS):
            landed(kind, c).wait_send()
            remote(
                o_part.at[kind, c, 1 - core], o_sib.at[kind, c], ss_sem.at[kind, c], sr_sem.at[2 + kind, c], sibling
            ).wait_send()


def deliver(*refs):
    sources, results, sem = refs[:5], refs[5:10], refs[10]
    copies = []
    for src, dst in zip(sources, results):
        parts = 1 if src.shape[0] == OWN else PARTS
        step = src.shape[0] // parts
        for lo in range(0, src.shape[0], step):
            rows = pl.ds(lo, step)
            copies.append(pltpu.make_async_copy(src.at[rows], dst.at[rows], sem.at[len(copies)]))
    for copy in copies:
        copy.start()
    for copy in copies:
        copy.wait()


def local(inputs, w_gate, w_up, w_down, cotangent):
    bf16, f32 = jnp.bfloat16, jnp.float32
    vmem = pltpu.VMEM
    scratch = [
        vmem((OWN, D), bf16),
        vmem((OWN, D), bf16),
        vmem((2, CHUNKS * HALF, D), bf16),
        vmem((2, CHUNKS * HALF, D), bf16),
        vmem((D, F), bf16),
        vmem((D, F), bf16),
        vmem((F, D), bf16),
        vmem((CHUNKS, 4, BLOCKS, ROWS, WIDE), bf16),
        vmem((CHUNKS, 4, BLOCKS - 1, ROWS, WIDE), bf16),
        vmem((CHUNKS, 4, BLOCKS, ROWS, WIDE), bf16),
        vmem((2, CHUNKS, 2, HALF, D), bf16),
        vmem((2, CHUNKS, HALF, D), bf16),
        vmem((2, CHUNKS * HALF, D), bf16),
        vmem((2, OWN, D), f32),
    ]
    for count in (BLOCKS, BLOCKS - 1, BLOCKS):
        scratch += [vmem((CHUNKS, count, ROWS, width), bf16) for _, width in SETS]
    dma = pltpu.SemaphoreType.DMA
    scratch += [
        dma((5,)), dma((10,)), dma((2, CHUNKS, 4, 4)), dma((2, CHUNKS)),
        dma((2, CHUNKS)), dma((4, CHUNKS)), dma((2, CHUNKS)), dma((4, CHUNKS)),
    ]
    whole = pl.BlockSpec(memory_space=pltpu.HBM)
    here = pl.BlockSpec(memory_space=pltpu.VMEM)
    results = (inputs, inputs, w_gate, w_up, w_down)
    held = pl.pallas_call(
        kernel,
        out_shape=tuple(pltpu.VMEM(a.shape, bf16) for a in results),
        in_specs=[whole] * 5,
        out_specs=[here] * 5,
        scratch_shapes=scratch,
        compiler_params=pltpu.CompilerParams(
            collective_id=0, has_side_effects=True, vmem_limit_bytes=40 * 2**20
        ),
    )(*[pltpu.with_memory_space_constraint(a, pltpu.HBM) for a in (inputs, w_gate, w_up, w_down, cotangent)])
    held = [pltpu.with_memory_space_constraint(a, pltpu.VMEM) for a in held]
    return pl.pallas_call(
        deliver,
        out_shape=tuple(jax.ShapeDtypeStruct(a.shape, bf16) for a in results),
        in_specs=[here] * 5,
        out_specs=[whole] * 5,
        scratch_shapes=[dma((2 + 3 * PARTS,))],
        compiler_params=pltpu.CompilerParams(vmem_limit_bytes=2**20),
    )(*held)


def solution(mesh):
    return jax.shard_map(
        local,
        mesh=mesh,
        in_specs=(P("col", "row"), P("row", "col"), P("row", "col"), P("col", "row"), P("col", "row")),
        out_specs=(P("col", "row"), P("col", "row"), P("row", "col"), P("row", "col"), P("col", "row")),
        check_vma=False,
    )
```

```python
import jax
import jax.numpy as jnp
from jax import lax
from jax.experimental import pallas as pl
from jax.experimental.pallas import tpu as pltpu
from jax.sharding import PartitionSpec as P

MESH = pl.DeviceIdType.MESH
ROWS = 16
OWN = 48
CHUNKS = 3
BLOCKS = 16
CHIPS = 8
SETS = ((0, 512), (512, 512), (1024, 384), (1408, 384))
D, F = 512, 1792
WIDE = 896
HALF = 128
PARTS = 4
BASE = (0, 8, 12, 14)

LAYOUT = (
    ((0, 0), (0, 1), (0, 2), (1, 0), (1, 1), (1, 2), (-1, 0), (-1, 1)),
    ((3, 1), (3, 2), (4, 0), (4, 1), (4, 2), (-3, 0), (-3, 1), (-3, 2)),
    ((3, 0), (2, 0), (2, 1), (-2, 0), (-2, 1), (2, 2), (-2, 2), (-1, 2)),
)
FAR = (1, -1, 2, -2, 3, 4, -3)
EARLY = 3
AHEAD = 5


def runs(c, first=0, count=8):
    found = []
    for i in range(first, first + count):
        d, part = LAYOUT[c][i]
        if found and found[-1][0] == d and found[-1][1] + found[-1][2] == part * ROWS:
            found[-1][2] += ROWS
        else:
            found.append([d, part * ROWS, ROWS, i * ROWS])
    return found


def back(d):
    return d if d == 4 else -d


contract_rows = (((0,), (0,)), ((), ()))
contract_cols = (((1,), (1,)), ((), ()))

ORDER = (
    ("c", 0), ("x", 0), ("ha", 3), ("ga", 0), ("ga", 1), ("ha", 0), ("ga", 3), ("ha", 2), ("ga", 2), ("ha", 1),
    ("sc", 0), ("c", 1), ("c", 2), ("hg", 0, 0), ("sx", 0), ("x", 1), ("hg", 0, 3), ("hg", 0, 1), ("hg", 0, 2),
    ("gu", 0, 1), ("gu", 0, 2), ("gu", 0, 0), ("gu", 0, 3), ("x", 2), ("r", 1, 0, 3, 1), ("k", 1, 0, 3, 1), ("r", 1,
    0, 0, 1), ("k", 1, 0, 0, 1), ("r", 1, 0, 2, 1), ("k", 1, 0, 2, 1), ("r", 1, 0, 1, 1), ("k", 1, 0, 1, 1), ("r",
    0, 0, 1, 1), ("k", 0, 0, 1, 1), ("r", 0, 0, 2, 1), ("sc", 1), ("k", 0, 0, 2, 1), ("r", 0, 0, 0, 1), ("k", 0, 0,
    0, 1), ("r", 0, 0, 3, 1), ("k", 0, 0, 3, 1), ("hg", 1, 1), ("r", 1, 0, 3, 2), ("r", 1, 0, 2, 2), ("k", 1, 0, 3,
    2), ("k", 1, 0, 2, 2), ("hg", 1, 2), ("hg", 1, 0), ("r", 1, 0, 0, 2), ("r", 1, 0, 1, 2), ("k", 1, 0, 0, 2),
    ("k", 1, 0, 1, 2), ("hg", 1, 3), ("sc", 2), ("hg", 2, 2), ("hg", 2, 3), ("hg", 2, 0), ("hg", 2, 1), ("r", 0, 0,
    1, 2), ("k", 0, 0, 1, 2), ("r", 0, 0, 2, 2), ("k", 0, 0, 2, 2), ("r", 1, 0, 2, 3), ("r", 0, 0, 0, 2), ("k", 0,
    0, 0, 2), ("k", 1, 0, 2, 3), ("r", 0, 0, 3, 2), ("k", 0, 0, 3, 2), ("r", 1, 0, 1, 3), ("k", 1, 0, 1, 3), ("sx",
    1), ("r", 1, 1, 2, 1), ("k", 1, 1, 2, 1), ("r", 1, 1, 1, 1), ("k", 1, 1, 1, 1), ("gu", 1, 0), ("r", 1, 0, 0, 3),
    ("r", 1, 0, 3, 3), ("k", 1, 0, 0, 3), ("k", 1, 0, 3, 3), ("gu", 1, 2), ("gu", 1, 3), ("sx", 2), ("gu", 1, 1),
    ("r", 1, 1, 0, 1), ("r", 1, 1, 3, 1), ("k", 1, 1, 0, 1), ("k", 1, 1, 3, 1), ("r", 1, 2, 3, 1), ("k", 1, 2, 3,
    1), ("gu", 2, 0), ("gu", 2, 3), ("gu", 2, 2), ("r", 0, 0, 3, 3), ("r", 0, 0, 2, 3), ("k", 0, 0, 2, 3), ("k", 0,
    0, 3, 3), ("gu", 2, 1), ("r", 0, 0, 0, 3), ("k", 0, 0, 0, 3), ("r", 1, 2, 2, 1), ("r", 1, 2, 0, 1), ("r", 0, 0,
    1, 3), ("k", 0, 0, 1, 3), ("r", 1, 2, 1, 1), ("k", 1, 2, 1, 1), ("k", 1, 2, 0, 1), ("k", 1, 2, 2, 1), ("r", 1,
    1, 2, 2), ("k", 1, 1, 2, 2), ("r", 1, 1, 1, 2), ("k", 1, 1, 1, 2), ("r", 0, 1, 2, 1), ("r", 0, 1, 3, 1), ("k",
    0, 1, 3, 1), ("k", 0, 1, 2, 1), ("r", 0, 1, 1, 1), ("k", 0, 1, 1, 1), ("r", 0, 1, 0, 1), ("k", 0, 1, 0, 1),
    ("r", 1, 1, 3, 2), ("k", 1, 1, 3, 2), ("r", 1, 1, 0, 2), ("k", 1, 1, 0, 2), ("r", 1, 2, 3, 2), ("k", 1, 2, 3,
    2), ("r", 0, 2, 0, 1), ("k", 0, 2, 0, 1), ("r", 0, 2, 1, 1), ("k", 0, 2, 1, 1), ("r", 0, 2, 3, 1), ("k", 0, 2,
    3, 1), ("r", 1, 2, 2, 2), ("mh", 0, 0), ("md", 0, 0), ("r", 0, 2, 2, 1), ("k", 0, 2, 2, 1), ("mh", 0, 1), ("md",
    0, 1), ("r", 1, 1, 2, 3), ("r", 1, 1, 1, 3), ("k", 1, 1, 2, 3), ("k", 1, 1, 1, 3), ("r", 1, 2, 1, 2), ("k", 1,
    2, 2, 2), ("k", 1, 2, 1, 2), ("r", 1, 2, 0, 2), ("k", 1, 2, 0, 2), ("r", 0, 1, 0, 2), ("k", 0, 1, 0, 2), ("r",
    0, 1, 3, 2), ("k", 0, 1, 3, 2), ("r", 0, 1, 1, 2), ("k", 0, 1, 1, 2), ("r", 0, 1, 2, 2), ("r", 1, 1, 0, 3),
    ("k", 0, 1, 2, 2), ("k", 1, 1, 0, 3), ("r", 1, 1, 3, 3), ("k", 1, 1, 3, 3), ("r", 1, 2, 3, 3), ("k", 1, 2, 3,
    3), ("r", 0, 0, 0, 5), ("r", 0, 2, 0, 2), ("k", 0, 2, 0, 2), ("r", 0, 0, 2, 5), ("r", 1, 0, 0, 5), ("r", 0, 2,
    1, 2), ("k", 0, 2, 1, 2), ("r", 0, 2, 3, 2), ("k", 0, 2, 3, 2), ("r", 1, 0, 2, 5), ("r", 1, 2, 2, 3), ("k", 1,
    2, 2, 3), ("r", 0, 0, 1, 5), ("r", 0, 0, 3, 5), ("r", 1, 2, 1, 3), ("k", 1, 2, 1, 3), ("r", 1, 0, 1, 5), ("r",
    1, 0, 3, 5), ("r", 1, 2, 0, 3), ("k", 1, 2, 0, 3), ("r", 0, 2, 2, 2), ("r", 0, 1, 3, 3), ("k", 0, 1, 3, 3),
    ("k", 0, 2, 2, 2), ("r", 0, 1, 0, 3), ("k", 0, 1, 0, 3), ("r", 0, 1, 2, 3), ("k", 0, 1, 2, 3), ("r", 0, 0, 0,
    6), ("r", 0, 1, 1, 3), ("k", 0, 1, 1, 3), ("r", 0, 0, 2, 6), ("r", 0, 2, 3, 3), ("k", 0, 2, 3, 3), ("r", 0, 2,
    0, 3), ("k", 0, 2, 0, 3), ("r", 0, 2, 1, 3), ("k", 0, 2, 1, 3), ("r", 0, 0, 3, 6), ("r", 1, 0, 2, 6), ("r", 0,
    0, 1, 6), ("r", 1, 0, 0, 6), ("r", 1, 0, 3, 6), ("r", 0, 2, 2, 3), ("k", 0, 2, 2, 3), ("r", 1, 0, 1, 6), ("mh",
    1, 1), ("md", 1, 1), ("mh", 1, 0), ("md", 1, 0), ("mh", 2, 1), ("r", 0, 0, 2, 7), ("r", 0, 0, 0, 7), ("md", 2,
    1), ("r", 0, 0, 3, 7), ("r", 0, 0, 1, 7), ("r", 1, 0, 0, 7), ("r", 1, 0, 2, 7), ("r", 1, 0, 3, 7), ("mh", 2, 0),
    ("r", 0, 1, 0, 5), ("r", 0, 1, 2, 5), ("r", 0, 1, 1, 5), ("md", 2, 0), ("r", 1, 0, 1, 7), ("r", 1, 1, 0, 5),
    ("r", 0, 1, 3, 5), ("r", 1, 1, 2, 5), ("r", 1, 1, 1, 5), ("r", 0, 2, 1, 5), ("r", 1, 1, 3, 5), ("r", 0, 2, 3,
    5), ("m3", 0), ("r", 0, 2, 2, 5), ("r", 1, 2, 2, 5), ("r", 1, 2, 1, 5), ("r", 1, 2, 3, 5), ("al", 0, 0), ("r",
    0, 2, 0, 5), ("r", 0, 1, 1, 6), ("r", 1, 2, 0, 5), ("m5", 0), ("r", 1, 1, 1, 6), ("r", 0, 1, 3, 6), ("r", 0, 1,
    0, 6), ("r", 0, 1, 2, 6), ("en", 0, 0), ("r", 1, 1, 0, 6), ("r", 1, 1, 2, 6), ("r", 0, 2, 1, 6), ("r", 1, 1, 3,
    6), ("r", 0, 2, 2, 6), ("al", 1, 0), ("r", 0, 2, 3, 6), ("r", 0, 2, 0, 6), ("r", 1, 2, 1, 6), ("r", 1, 2, 2, 6),
    ("r", 1, 2, 3, 6), ("r", 0, 1, 1, 7), ("r", 1, 2, 0, 6), ("r", 0, 1, 3, 7), ("r", 0, 1, 2, 7), ("r", 0, 1, 0,
    7), ("en", 1, 0), ("r", 1, 1, 1, 7), ("r", 1, 1, 3, 7), ("r", 1, 1, 2, 7), ("r", 1, 1, 0, 7), ("r", 0, 2, 1, 7),
    ("r", 0, 2, 3, 7), ("r", 0, 2, 2, 7), ("r", 0, 2, 0, 7), ("r", 1, 2, 1, 7), ("r", 1, 2, 3, 7), ("r", 1, 2, 2,
    7), ("m3", 1), ("r", 1, 2, 0, 7), ("al", 0, 1), ("m5", 1), ("al", 1, 1), ("m3", 2), ("m4", 1), ("m4", 0), ("al",
    0, 2), ("m4", 2), ("en", 0, 1), ("m4", 3), ("m5", 2), ("m5", 3), ("al", 1, 2), ("m6", 1), ("al", 1, 3), ("m6",
    2), ("m6", 3), ("m6", 0), ("en", 1, 1), ("en", 0, 2), ("en", 1, 2),
)


def place(turn, block):
    bits = [(block >> (3 - d)) & 1 for d in range(4)]
    index = 0
    for step in range(4):
        index = index * 2 + bits[(turn + step) % 4]
    return index


PLACES = [[place(j, i) for i in range(8)] for j in range(4)]


def at(turn, core, i):
    return PLACES[turn][i] if core == 0 else BLOCKS - 1 - PLACES[turn][i]


def kernel(
    x_hbm, wg_hbm, wu_hbm, wd_hbm, ct_hbm,
    out, ig, gg, ug, dg,
    x_in, ct_in, xs, cts, wg, wu, wd,
    p_gu, r_gu, d_all, o_part, o_sib, o_z, o_sum,
    p_h0, p_h1, p_h2, p_h3, r_h0, r_h1, r_h2, r_h3, h0, h1, h2, h3,
    load_sem, ssem, rsem, last_sem, zs_sem, zr_sem, ss_sem, sr_sem,
):
    p_hg, r_hg, h_all = (p_h0, p_h1, p_h2, p_h3), (r_h0, r_h1, r_h2, r_h3), (h0, h1, h2, h3)
    row, col = lax.axis_index("row"), lax.axis_index("col")
    y, x = row // 4, row % 4
    z, core = col // 2, col % 2
    partner = (
        (y * 4 + x + 1 - 2 * (x % 2), col),
        ((y + 1 - 2 * (y % 2)) * 4 + x, col),
        (y * 4 + 3 - x, col),
        ((3 - y) * 4 + x, col),
    )
    bits = (((x + 1) // 2) % 2, ((y + 1) // 2) % 2, x // 2, y // 2)
    mine = []
    for turn in range(4):
        index = 0
        for step in range(4):
            index = index * 2 + bits[(turn + step) % 4]
        mine.append(index)
    sibling = (row, z * 2 + 1 - core)
    along = {d: (row, lax.rem(z + d * (1 - 2 * core) + CHIPS, CHIPS) * 2 + core) for d in FAR}

    loads = []
    for i, (src, dst) in enumerate(
        ((x_hbm, x_in), (ct_hbm, ct_in), (wg_hbm, wg), (wu_hbm, wu), (wd_hbm, wd))
    ):
        loads.append(pltpu.make_async_copy(src, dst, load_sem.at[i]))
        loads[-1].start()

    barrier = pltpu.get_barrier_semaphore()
    peers = list(along.values()) + list(partner) + [sibling]
    for peer in peers:
        pl.semaphore_signal(barrier, inc=1, device_id=peer, device_id_type=MESH)
    loads[0].wait()
    loads[1].wait()
    pl.semaphore_wait(barrier, len(peers))

    def remote(src, dst, send_sem, recv_sem, device):
        return pltpu.make_async_remote_copy(
            src_ref=src, dst_ref=dst, send_sem=send_sem, recv_sem=recv_sem,
            device_id=device, device_id_type=MESH,
        )

    stores, sources = (xs, cts), (x_in, ct_in)
    first_done = set()

    def once(key, act):
        if key not in first_done:
            first_done.add(key)
            act()

    def region(kind, who, group):
        if group == 3:
            return stores[kind].at[who, pl.ds(0, OWN)]
        lo = OWN if group == 0 else group * HALF
        return stores[kind].at[who, pl.ds(lo, (group + 1) * HALF - lo)]

    def gather_start(kind, group):
        own = sources[kind]
        if group == 0:
            spot = region(kind, core, 3)
            remote(own, spot, ss_sem.at[kind, 3], sr_sem.at[kind, 3], sibling).start()
        for d, lo, count, first in runs(group):
            if d != 0:
                remote(
                    own.at[pl.ds(lo, count)], stores[kind].at[core, pl.ds(group * HALF + first, count)],
                    zs_sem.at[kind, group], zr_sem.at[kind, group], along[back(d)],
                ).start()
        if group == 0:
            spot[...] = own[...]

    def gather_share(kind, group):
        whole = region(kind, core, group)
        remote(whole, whole, zs_sem.at[kind, group], zr_sem.at[kind, group], sibling).wait_recv()
        remote(whole, whole, ss_sem.at[kind, group], sr_sem.at[kind, group], sibling).start()

    def gather_end(kind, group):
        def act():
            whole = region(kind, 1 - core, group)
            remote(whole, whole, ss_sem.at[kind, group], sr_sem.at[kind, group], sibling).wait_recv()
        once(("gathered", kind, group), act)

    def gather_sent(kind, group):
        whole = region(kind, core, group)
        if group < 3:
            remote(whole, whole, zs_sem.at[kind, group], zr_sem.at[kind, group], sibling).wait_send()
        remote(whole, whole, ss_sem.at[kind, group], sr_sem.at[kind, group], sibling).wait_send()

    def rows_of(buffer, c):
        return buffer[:, c * HALF:(c + 1) * HALF, :].reshape(2 * HALF, D)

    def turn_of(lane, j, step):
        return (j + 2) % 4 if lane == 1 and step < 4 else j

    def dim_of(lane, j, step):
        turn = turn_of(lane, j, step)
        return (turn + step) % 4 if step < 4 else (turn + 7 - step) % 4

    def ends(lane, c, j, step):
        own = mine[turn_of(lane, j, step)]
        if step < 4:
            part, arrive = (p_gu.at[c, j], r_gu.at[c, j]) if lane == 0 else (p_hg[j].at[c], r_hg[j].at[c])
            half = 8 >> step
            keep = own // half * half
            give = keep + half - 2 * half * (own // half % 2)
            return part.at[pl.ds(give, half)], arrive.at[pl.ds(BASE[step], half)]
        buffer = h_all[j].at[c] if lane == 0 else d_all.at[c, j]
        size = 1 << (step - 4)
        region = buffer.at[pl.ds(own // size * size, size)]
        return region, region

    SLOT = (0, 1, 2, 3, 2, 1, 0)

    def semaphores(lane, c, j, step):
        if lane == 0:
            leaving = ssem.at[0] if step < 4 else ssem.at[1 + j]
        else:
            leaving = ssem.at[5 + j] if step < 4 else ssem.at[9]
        coming = last_sem.at[lane * CHUNKS + c] if step == 7 else rsem.at[lane, c, turn_of(lane, j, step), SLOT[step]]
        return leaving, coming

    def copy_of(lane, c, j, step):
        return remote(
            *ends(lane, c, j, step), *semaphores(lane, c, j, step), partner[dim_of(lane, j, step)]
        )

    def launch(lane, c, j, step):
        if (lane, c, step) != (1, 2, 7):
            copy_of(lane, c, j, step).start()
            return
        high = mine[j] // 8
        for i in range(8):
            p = PLACES[j][i]
            block = d_all.at[c, j, pl.ds(p + (high if p < 8 else 1 - high) * (15 - 2 * p), 1)]
            leaving, coming = semaphores(lane, c, j, step)
            if i >= AHEAD:
                coming = last_sem.at[2 * CHUNKS]
            remote(block, block, leaving, coming, partner[dim_of(lane, j, step)]).start()

    def launch_blocks(lane, j, first, count):
        part, arrive = (p_gu.at[0, j], r_gu.at[0, j]) if lane == 0 else (p_hg[j].at[0], r_hg[j].at[0])
        turn = turn_of(lane, j, 0)
        high = mine[turn] // 8
        for i in range(first, first + count):
            p = PLACES[turn][i]
            q = p + (1 - high if p < 8 else high) * (15 - 2 * p)
            remote(
                part.at[pl.ds(q, 1)], arrive.at[pl.ds(q - 8 * (1 - high), 1)],
                *semaphores(lane, 0, j, 0), partner[dim_of(lane, j, 0)],
            ).start()

    def arrived(lane, c, j, step):
        if step < 4:
            copy_of(lane, c, j, step).wait_recv()
        else:
            own = mine[j]
            size = 1 << (step - 4)
            buffer = h_all[j].at[c] if lane == 0 else d_all.at[c, j]
            keep = own // size * size
            other = buffer.at[pl.ds(keep + size - 2 * size * (own // size % 2), size)]
            remote(
                other, other, *semaphores(lane, c, j, step), partner[dim_of(lane, j, step)]
            ).wait_recv()

    def add_arrived(lane, c, j, step, given):
        part, arrive = (p_gu.at[c, j], r_gu.at[c, j]) if lane == 0 else (p_hg[j].at[c], r_hg[j].at[c])
        index = mine[turn_of(lane, j, step)]
        half, wide = 8 >> step, 16 >> step
        start = index // wide * wide
        keep = index // half * half
        give = keep + half - 2 * half * (index // half % 2)

        first = give if given else keep

        def body(i, carry):
            where = first + i
            part[where] = (
                part[where].astype(jnp.float32) + arrive[BASE[step - 1] + where - start].astype(jnp.float32)
            ).astype(jnp.bfloat16)
            return carry

        lax.fori_loop(0, half, body, 0)

    def reduce_step(lane, c, j, step):
        arrived(lane, c, j, step - 1)
        add_arrived(lane, c, j, step, True)
        launch(lane, c, j, step)

    def reduce_rest(lane, c, j, step):
        add_arrived(lane, c, j, step, False)

    def total_of(lane, c, j):
        part, arrive = (p_gu.at[c, j], r_gu.at[c, j]) if lane == 0 else (p_hg[j].at[c], r_hg[j].at[c])
        return part[mine[turn_of(lane, j, 0)]].astype(jnp.float32) + arrive[BASE[3]].astype(jnp.float32)

    def store_partial(ref, turn, lo, value, first, count):
        width = value.shape[1]
        value = value.astype(jnp.bfloat16)
        for k in range(2 * count):
            ref[at(turn, k // count, first + k % count), :, lo:lo + width] = value[k * ROWS:(k + 1) * ROWS, :]

    def some_rows(buffer, c, first, count):
        lo = c * HALF + first * ROWS
        return buffer[:, lo:lo + count * ROWS, :].reshape(2 * count * ROWS, D)

    def gate_up_product(c, j, first, count):
        once("w_gate", loads[2].wait)
        once("w_up", loads[3].wait)
        value = some_rows(xs, c, first, count)
        ref, start = p_gu.at[c, j], 0
        for weight, (lo, width) in ((wg, SETS[j]), (wu, SETS[(j + 2) % 4])):
            term = jnp.dot(value, weight[:, lo:lo + width], preferred_element_type=jnp.float32)
            store_partial(ref, j, start, term, first, count)
            start += width

    def hidden_grad_product(c, j, first, count):
        once("w_down", loads[4].wait)
        lo, width = SETS[j]
        value = some_rows(cts, c, first, count)
        term = lax.dot_general(value, wd[lo:lo + width, :], contract_cols, preferred_element_type=jnp.float32)
        store_partial(p_hg[j].at[c], (j + 2) % 4, 0, term, first, count)

    def gate_up_early(j):
        gather_end(0, 3)
        gate_up_product(0, j, 0, EARLY)
        launch_blocks(0, j, 0, EARLY)

    def hidden_grad_early(j):
        gather_end(1, 3)
        hidden_grad_product(0, j, 0, EARLY)
        launch_blocks(1, j, 0, EARLY)

    def gate_up(c, j):
        gather_end(0, c)
        if c == 0:
            gate_up_product(0, j, EARLY, 8 - EARLY)
            launch_blocks(0, j, EARLY, 8 - EARLY)
        else:
            gate_up_product(c, j, 0, 8)
            launch(0, c, j, 0)

    def hidden_grad(c, j):
        gather_end(1, c)
        if c == 0:
            hidden_grad_product(0, j, EARLY, 8 - EARLY)
            launch_blocks(1, j, EARLY, 8 - EARLY)
        else:
            hidden_grad_product(c, j, 0, 8)
            launch(1, c, j, 0)

    def make_hidden(c, pair):
        streams = (pair, pair + 2)
        for j in streams:
            arrived(0, c, j, 3)
        sums = {j: total_of(0, c, j) for j in streams}
        for j in streams:
            width = SETS[j][1]
            gate = sums[j][:, :width]
            up = sums[(j + 2) % 4][:, WIDE - width:]
            h_all[j][c, mine[j]] = (gate * jax.nn.sigmoid(gate) * up).astype(jnp.bfloat16)
            launch(0, c, j, 4)

    def make_deltas(c, pair):
        streams = (pair, pair + 2)
        for j in streams:
            arrived(1, c, j, 3)
        sums = {j: total_of(0, c, j) for j in streams}
        for j in streams:
            other = (j + 2) % 4
            width = SETS[j][1]
            gate = sums[j][:, :width]
            up = sums[other][:, WIDE - width:]
            grad = total_of(1, c, j)
            s = jax.nn.sigmoid(gate)
            d_all[c, j, mine[j], :, :width] = (grad * up * s * (1.0 + gate * (1.0 - s))).astype(jnp.bfloat16)
            d_all[c, other, mine[other], :, WIDE - width:] = (grad * gate * s).astype(jnp.bfloat16)
        for j in streams:
            launch(1, c, j, 4)

    def tokens(ref, c, j, lo, width, first=0, count=8):
        blocks = [ref[c, at(j, k // count, first + k % count), :, lo:lo + width] for k in range(2 * count)]
        return jnp.concatenate(blocks, axis=0)

    def hidden_of(c, j):
        return tokens(h_all[j], c, j, 0, SETS[j][1])

    def gate_delta_of(c, j, *some):
        return tokens(d_all.at[:, j], c, j, 0, SETS[j][1], *some)

    def up_delta_of(c, j, *some):
        other = (j + 2) % 4
        return tokens(d_all.at[:, other], c, other, WIDE - SETS[j][1], SETS[j][1], *some)

    def gathered(lane, c, ahead=False):
        def act(size, sem):
            remote(size, size, ssem.at[1], last_sem.at[sem], sibling).wait_recv()

        split = (lane, c) == (1, 2)
        if lane == 0:
            size = p_gu.at[c, 0]
        else:
            size = d_all.at[c, :, pl.ds(0, AHEAD if split else 8)]
        once(("doubled", lane, c), lambda: act(size, lane * CHUNKS + c))
        if split and not ahead:
            once("rest", lambda: act(d_all.at[c, :, pl.ds(0, 8 - AHEAD)], 2 * CHUNKS))

    def share_of(kind, c, first, count):
        rows = pl.ds(first * ROWS, count * ROWS)
        slot = c if first == 0 else 3
        return remote(
            o_part.at[kind, c, 1 - core, rows], o_sib.at[kind, c, rows],
            ss_sem.at[kind, slot], sr_sem.at[2 + kind, slot], sibling,
        )

    def scatter_start(kind, c, total, first=0, count=8):
        rows = count * ROWS
        o_part[kind, c, :, first * ROWS:first * ROWS + rows, :] = total.astype(jnp.bfloat16).reshape(2, rows, D)
        once(("sent", kind, c, first), lambda: gather_sent(kind, c if first == 0 else 3))
        share_of(kind, c, first, count).start()

    def scatter_along(kind, c, first=0, count=8):
        share_of(kind, c, first, count).wait_recv()
        lo, hi = first * ROWS, (first + count) * ROWS
        o_part[kind, c, core, lo:hi, :] = (
            o_part[kind, c, core, lo:hi, :].astype(jnp.float32) + o_sib[kind, c, lo:hi, :].astype(jnp.float32)
        ).astype(jnp.bfloat16)
        for d, row, rows, start in runs(c, first, count):
            if d != 0:
                remote(
                    o_part.at[kind, c, core, pl.ds(start, rows)],
                    o_z.at[kind, pl.ds(FAR.index(back(d)) * OWN + row, rows)],
                    zs_sem.at[kind, c], zr_sem.at[2 + kind, c], along[d],
                ).start()

    def landed(kind, c):
        whole = o_z.at[kind, pl.ds(0, HALF - (OWN if c == 0 else 0))]
        return remote(whole, whole, zs_sem.at[kind, c], zr_sem.at[2 + kind, c], sibling)

    def scatter_end(kind, c):
        landed(kind, c).wait_recv()
        for d, row, rows, start in runs(c):
            if d == 0:
                o_sum[kind] = o_part[kind, c, core, 0:OWN, :].astype(jnp.float32)
            else:
                spot = FAR.index(back(d)) * OWN + row
                o_sum[kind, row:row + rows, :] += o_z[kind, spot:spot + rows, :].astype(jnp.float32)
        if c == CHUNKS - 1:
            (out, ig)[kind][...] = o_sum[kind].astype(jnp.bfloat16)

    def output_part(c):
        gathered(0, c)
        total = None
        for j in range(4):
            lo, width = SETS[j]
            term = jnp.dot(hidden_of(c, j), wd[lo:lo + width, :], preferred_element_type=jnp.float32)
            total = term if total is None else total + term
        scatter_start(0, c, total)

    def input_grad_part(c):
        split = c >= CHUNKS - 1
        some = (((0, AHEAD), (AHEAD, 8 - AHEAD))[c - 2]) if split else (0, 8)
        gathered(1, min(c, 2), c == 2)
        total = None
        for j in range(4):
            lo, width = SETS[j]
            term = lax.dot_general(
                gate_delta_of(min(c, 2), j, *some), wg[:, lo:lo + width], contract_cols,
                preferred_element_type=jnp.float32,
            ) + lax.dot_general(
                up_delta_of(min(c, 2), j, *some), wu[:, lo:lo + width], contract_cols,
                preferred_element_type=jnp.float32,
            )
            total = term if total is None else total + term
        scatter_start(1, min(c, 2), total, *some)

    def along_part(kind, c):
        if kind == 1 and c >= CHUNKS - 1:
            scatter_along(1, 2, *((0, AHEAD), (AHEAD, 8 - AHEAD))[c - 2])
        else:
            scatter_along(kind, c)

    def over_tokens(left, right):
        a = jnp.concatenate([left(c) for c in range(CHUNKS)], axis=0)
        b = jnp.concatenate([right(c) for c in range(CHUNKS)], axis=0)
        return lax.dot_general(a, b, contract_rows, preferred_element_type=jnp.float32).astype(jnp.bfloat16)

    def down_grad(j):
        for c in range(CHUNKS):
            gathered(0, c)
        lo, width = SETS[j]
        dg[lo:lo + width, :] = over_tokens(lambda c: hidden_of(c, j), lambda c: rows_of(cts, c))

    def input_side_grads(j):
        for c in range(CHUNKS):
            gathered(1, c)
        lo, width = SETS[j]
        for res, of in ((gg, gate_delta_of), (ug, up_delta_of)):
            res[:, lo:lo + width] = over_tokens(lambda c: rows_of(xs, c), lambda c: of(c, j))

    def halve_or_double(lane, c, j, step):
        if step < 4:
            reduce_step(lane, c, j, step)
        else:
            arrived(lane, c, j, step - 1)
            launch(lane, c, j, step)

    acts = {
        "x": lambda c: gather_start(0, c), "c": lambda c: gather_start(1, c),
        "sx": lambda c: gather_share(0, c), "sc": lambda c: gather_share(1, c),
        "gu": gate_up, "hg": hidden_grad, "r": halve_or_double, "k": reduce_rest, "mh": make_hidden, "md": make_deltas,
        "m3": output_part, "m5": input_grad_part, "al": along_part, "ga": gate_up_early, "ha": hidden_grad_early, "en": scatter_end,
        "m4": down_grad, "m6": input_side_grads,
    }
    for act, *where in ORDER:
        acts[act](*where)

    left = [(r_gu, 0)]
    for j in range(4):
        left += [(h_all[j].at[:, pl.ds(0, BLOCKS - 1)], 1 + j), (r_hg[j], 5 + j)]
    left.append((d_all.at[:, :, pl.ds(0, BLOCKS - 1)], 9))
    for size, i in left:
        remote(size, size, ssem.at[i], last_sem.at[0], sibling).wait_send()
    gather_sent(0, 3)
    for kind in range(2):
        for c in range(CHUNKS):
            landed(kind, c).wait_send()
            if (kind, c) == (1, 2):
                share_of(1, 2, 0, AHEAD).wait_send()
                share_of(1, 2, AHEAD, 8 - AHEAD).wait_send()
            else:
                share_of(kind, c, 0, 8).wait_send()


def deliver(*refs):
    sources, results, sem = refs[:5], refs[5:10], refs[10]
    copies = []
    for src, dst in zip(sources, results):
        parts = 1 if src.shape[0] == OWN else PARTS
        step = src.shape[0] // parts
        for lo in range(0, src.shape[0], step):
            rows = pl.ds(lo, step)
            copies.append(pltpu.make_async_copy(src.at[rows], dst.at[rows], sem.at[len(copies)]))
    for copy in copies:
        copy.start()
    for copy in copies:
        copy.wait()


def local(inputs, w_gate, w_up, w_down, cotangent):
    bf16, f32 = jnp.bfloat16, jnp.float32
    vmem = pltpu.VMEM
    scratch = [
        vmem((OWN, D), bf16),
        vmem((OWN, D), bf16),
        vmem((2, CHUNKS * HALF, D), bf16),
        vmem((2, CHUNKS * HALF, D), bf16),
        vmem((D, F), bf16),
        vmem((D, F), bf16),
        vmem((F, D), bf16),
        vmem((CHUNKS, 4, BLOCKS, ROWS, WIDE), bf16),
        vmem((CHUNKS, 4, BLOCKS - 1, ROWS, WIDE), bf16),
        vmem((CHUNKS, 4, BLOCKS, ROWS, WIDE), bf16),
        vmem((2, CHUNKS, 2, HALF, D), bf16),
        vmem((2, CHUNKS, HALF, D), bf16),
        vmem((2, len(FAR) * OWN, D), bf16),
        vmem((2, OWN, D), f32),
    ]
    for count in (BLOCKS, BLOCKS - 1, BLOCKS):
        scratch += [vmem((CHUNKS, count, ROWS, width), bf16) for _, width in SETS]
    dma = pltpu.SemaphoreType.DMA
    scratch += [
        dma((5,)), dma((10,)), dma((2, CHUNKS, 4, 4)), dma((2 * CHUNKS + 1,)),
        dma((2, CHUNKS)), dma((4, CHUNKS)), dma((2, 4)), dma((4, 4)),
    ]
    whole = pl.BlockSpec(memory_space=pltpu.HBM)
    here = pl.BlockSpec(memory_space=pltpu.VMEM)
    results = (inputs, inputs, w_gate, w_up, w_down)
    held = pl.pallas_call(
        kernel,
        out_shape=tuple(pltpu.VMEM(a.shape, bf16) for a in results),
        in_specs=[whole] * 5,
        out_specs=[here] * 5,
        scratch_shapes=scratch,
        compiler_params=pltpu.CompilerParams(
            collective_id=0, has_side_effects=True, vmem_limit_bytes=40 * 2**20
        ),
    )(*[pltpu.with_memory_space_constraint(a, pltpu.HBM) for a in (inputs, w_gate, w_up, w_down, cotangent)])
    held = [pltpu.with_memory_space_constraint(a, pltpu.VMEM) for a in held]
    return pl.pallas_call(
        deliver,
        out_shape=tuple(jax.ShapeDtypeStruct(a.shape, bf16) for a in results),
        in_specs=[here] * 5,
        out_specs=[whole] * 5,
        scratch_shapes=[dma((2 + 3 * PARTS,))],
        compiler_params=pltpu.CompilerParams(vmem_limit_bytes=2**20),
    )(*held)


def solution(mesh):
    return jax.shard_map(
        local,
        mesh=mesh,
        in_specs=(P("col", "row"), P("row", "col"), P("row", "col"), P("col", "row"), P("col", "row")),
        out_specs=(P("col", "row"), P("col", "row"), P("row", "col"), P("row", "col"), P("col", "row")),
        check_vma=False,
    )
```

```python
import jax
import jax.numpy as jnp
from jax import lax
from jax.experimental import pallas as pl
from jax.experimental.pallas import tpu as pltpu
from jax.sharding import PartitionSpec as P

MESH = pl.DeviceIdType.MESH
ROWS = 16
OWN = 48
CHUNKS = 3
BLOCKS = 16
CHIPS = 8
SETS = ((0, 512), (512, 512), (1024, 384), (1408, 384))
D, F = 512, 1792
WIDE = 896
HALF = 128
PARTS = 4
BASE = (0, 8, 12, 14)

LAYOUT = (
    ((0, 0), (0, 1), (0, 2), (1, 0), (1, 1), (1, 2), (-1, 0), (-1, 1)),
    ((3, 1), (3, 2), (4, 0), (4, 1), (4, 2), (-3, 0), (-3, 1), (-3, 2)),
    ((3, 0), (2, 0), (2, 1), (-2, 0), (-2, 1), (2, 2), (-2, 2), (-1, 2)),
)
FAR = (1, -1, 2, -2, 3, 4, -3)
EARLY = 3
AHEAD = 5


def runs(c, first=0, count=8):
    found = []
    for i in range(first, first + count):
        d, part = LAYOUT[c][i]
        if found and found[-1][0] == d and found[-1][1] + found[-1][2] == part * ROWS:
            found[-1][2] += ROWS
        else:
            found.append([d, part * ROWS, ROWS, i * ROWS])
    return found


def back(d):
    return d if d == 4 else -d


contract_rows = (((0,), (0,)), ((), ()))
contract_cols = (((1,), (1,)), ((), ()))

ORDER = (
    ("x", 0), ("c", 0), ("ga", 0), ("ha", 0), ("ha", 2), ("ha", 3), ("ga", 3), ("ha", 1), ("ga", 2), ("ga", 1),
    ("sx", 0), ("x", 1), ("x", 2), ("sc", 0), ("c", 1), ("c", 2), ("gu", 0, 2), ("gu", 0, 3), ("gu", 0, 1), ("hg",
    0, 3), ("hg", 0, 1), ("gu", 0, 0), ("hg", 0, 0), ("hg", 0, 2), ("r", 0, 0, 2, 1), ("k", 0, 0, 2, 1), ("r", 0, 0,
    3, 1), ("k", 0, 0, 3, 1), ("r", 0, 0, 1, 1), ("k", 0, 0, 1, 1), ("sx", 1), ("r", 0, 0, 0, 1), ("k", 0, 0, 0, 1),
    ("r", 1, 0, 0, 1), ("k", 1, 0, 0, 1), ("r", 1, 0, 3, 1), ("k", 1, 0, 3, 1), ("r", 1, 0, 1, 1), ("k", 1, 0, 1,
    1), ("gu", 1, 0), ("r", 1, 0, 2, 1), ("k", 1, 0, 2, 1), ("gu", 1, 3), ("gu", 1, 2), ("gu", 1, 1), ("sx", 2),
    ("gu", 2, 3), ("r", 0, 0, 2, 2), ("r", 0, 0, 3, 2), ("k", 0, 0, 3, 2), ("k", 0, 0, 2, 2), ("gu", 2, 2), ("r", 0,
    0, 1, 2), ("k", 0, 0, 1, 2), ("gu", 2, 0), ("r", 1, 0, 0, 2), ("r", 0, 0, 0, 2), ("k", 1, 0, 0, 2), ("k", 0, 0,
    0, 2), ("gu", 2, 1), ("r", 1, 0, 3, 2), ("r", 1, 0, 1, 2), ("k", 1, 0, 3, 2), ("k", 1, 0, 1, 2), ("r", 1, 0, 2,
    2), ("k", 1, 0, 2, 2), ("sc", 1), ("hg", 1, 1), ("hg", 1, 0), ("hg", 1, 2), ("hg", 1, 3), ("sc", 2), ("r", 0, 1,
    3, 1), ("k", 0, 1, 3, 1), ("r", 0, 1, 2, 1), ("k", 0, 1, 2, 1), ("r", 0, 1, 0, 1), ("k", 0, 1, 0, 1), ("hg", 2,
    3), ("hg", 2, 1), ("r", 0, 1, 1, 1), ("k", 0, 1, 1, 1), ("hg", 2, 0), ("r", 0, 0, 2, 3), ("k", 0, 0, 2, 3),
    ("hg", 2, 2), ("r", 0, 0, 3, 3), ("k", 0, 0, 3, 3), ("r", 0, 2, 3, 1), ("k", 0, 2, 3, 1), ("r", 0, 2, 2, 1),
    ("k", 0, 2, 2, 1), ("r", 0, 0, 1, 3), ("k", 0, 0, 1, 3), ("r", 0, 0, 0, 3), ("k", 0, 0, 0, 3), ("r", 0, 2, 0,
    1), ("k", 0, 2, 0, 1), ("r", 1, 0, 3, 3), ("k", 1, 0, 3, 3), ("r", 1, 0, 2, 3), ("k", 1, 0, 2, 3), ("r", 1, 0,
    0, 3), ("k", 1, 0, 0, 3), ("r", 0, 2, 1, 1), ("k", 0, 2, 1, 1), ("r", 1, 0, 1, 3), ("k", 1, 0, 1, 3), ("r", 1,
    1, 2, 1), ("k", 1, 1, 2, 1), ("r", 1, 1, 1, 1), ("k", 1, 1, 1, 1), ("r", 1, 1, 0, 1), ("k", 1, 1, 0, 1), ("r",
    1, 1, 3, 1), ("k", 1, 1, 3, 1), ("r", 0, 1, 3, 2), ("k", 0, 1, 3, 2), ("r", 0, 1, 2, 2), ("k", 0, 1, 2, 2),
    ("r", 0, 1, 1, 2), ("k", 0, 1, 1, 2), ("r", 0, 1, 0, 2), ("k", 0, 1, 0, 2), ("r", 1, 2, 2, 1), ("k", 1, 2, 2,
    1), ("r", 1, 2, 3, 1), ("k", 1, 2, 3, 1), ("r", 1, 2, 1, 1), ("k", 1, 2, 1, 1), ("r", 1, 2, 0, 1), ("k", 1, 2,
    0, 1), ("r", 0, 2, 3, 2), ("k", 0, 2, 3, 2), ("mh", 0, 1), ("r", 0, 2, 2, 2), ("k", 0, 2, 2, 2), ("r", 0, 2, 0,
    2), ("k", 0, 2, 0, 2), ("mh", 0, 0), ("md", 0, 0), ("r", 0, 2, 1, 2), ("k", 0, 2, 1, 2), ("md", 0, 1), ("r", 1,
    1, 1, 2), ("k", 1, 1, 1, 2), ("r", 1, 1, 2, 2), ("k", 1, 1, 2, 2), ("r", 1, 1, 0, 2), ("k", 1, 1, 0, 2), ("r",
    1, 1, 3, 2), ("k", 1, 1, 3, 2), ("r", 0, 1, 2, 3), ("k", 0, 1, 2, 3), ("r", 0, 1, 3, 3), ("k", 0, 1, 3, 3),
    ("r", 0, 1, 1, 3), ("k", 0, 1, 1, 3), ("r", 0, 1, 0, 3), ("k", 0, 1, 0, 3), ("r", 1, 2, 1, 2), ("k", 1, 2, 1,
    2), ("r", 1, 2, 2, 2), ("k", 1, 2, 2, 2), ("r", 0, 0, 1, 5), ("r", 1, 2, 3, 2), ("k", 1, 2, 3, 2), ("r", 0, 0,
    3, 5), ("r", 1, 2, 0, 2), ("k", 1, 2, 0, 2), ("r", 0, 0, 0, 5), ("r", 0, 2, 3, 3), ("k", 0, 2, 3, 3), ("r", 0,
    2, 2, 3), ("k", 0, 2, 2, 3), ("r", 0, 0, 2, 5), ("r", 1, 0, 0, 5), ("r", 0, 2, 0, 3), ("k", 0, 2, 0, 3), ("r",
    1, 0, 1, 5), ("r", 1, 0, 2, 5), ("r", 1, 0, 3, 5), ("r", 1, 1, 0, 3), ("k", 1, 1, 0, 3), ("r", 1, 1, 1, 3),
    ("r", 0, 2, 1, 3), ("k", 1, 1, 1, 3), ("k", 0, 2, 1, 3), ("r", 1, 1, 2, 3), ("k", 1, 1, 2, 3), ("r", 1, 1, 3,
    3), ("k", 1, 1, 3, 3), ("mh", 1, 1), ("mh", 1, 0), ("r", 1, 2, 2, 3), ("k", 1, 2, 2, 3), ("r", 1, 2, 1, 3),
    ("k", 1, 2, 1, 3), ("r", 1, 2, 0, 3), ("k", 1, 2, 0, 3), ("r", 0, 0, 3, 6), ("r", 0, 0, 1, 6), ("r", 0, 0, 0,
    6), ("r", 1, 2, 3, 3), ("r", 0, 0, 2, 6), ("k", 1, 2, 3, 3), ("mh", 2, 0), ("r", 1, 0, 2, 6), ("r", 1, 0, 0, 6),
    ("r", 1, 0, 3, 6), ("r", 1, 0, 1, 6), ("mh", 2, 1), ("r", 0, 1, 3, 5), ("md", 1, 0), ("r", 0, 1, 2, 5), ("md",
    1, 1), ("r", 0, 1, 0, 5), ("r", 0, 1, 1, 5), ("md", 2, 0), ("r", 0, 0, 3, 7), ("md", 2, 1), ("r", 0, 0, 1, 7),
    ("r", 0, 0, 2, 7), ("r", 0, 0, 0, 7), ("r", 0, 2, 2, 5), ("r", 0, 2, 0, 5), ("r", 1, 0, 2, 7), ("r", 1, 0, 0,
    7), ("r", 1, 0, 3, 7), ("r", 1, 0, 1, 7), ("r", 0, 2, 1, 5), ("r", 0, 1, 3, 6), ("r", 1, 1, 0, 5), ("r", 0, 2,
    3, 5), ("r", 0, 1, 2, 6), ("r", 1, 1, 2, 5), ("r", 1, 1, 3, 5), ("r", 0, 1, 1, 6), ("r", 1, 1, 1, 5), ("r", 1,
    2, 2, 5), ("r", 1, 2, 0, 5), ("r", 0, 1, 0, 6), ("r", 1, 2, 1, 5), ("r", 1, 2, 3, 5), ("m3", 0), ("r", 0, 2, 0,
    6), ("r", 0, 2, 2, 6), ("al", 0, 0), ("r", 0, 2, 1, 6), ("r", 0, 2, 3, 6), ("m5", 0), ("r", 1, 1, 0, 6), ("r",
    1, 1, 3, 6), ("r", 1, 1, 1, 6), ("r", 0, 1, 2, 7), ("r", 0, 1, 3, 7), ("en", 0, 0), ("r", 0, 1, 0, 7), ("r", 1,
    1, 2, 6), ("r", 0, 1, 1, 7), ("r", 1, 2, 1, 6), ("al", 1, 0), ("r", 1, 2, 3, 6), ("r", 1, 2, 2, 6), ("r", 1, 2,
    0, 6), ("r", 0, 2, 2, 7), ("r", 0, 2, 3, 7), ("r", 0, 2, 0, 7), ("r", 0, 2, 1, 7), ("en", 1, 0), ("r", 1, 1, 3,
    7), ("r", 1, 1, 0, 7), ("r", 1, 1, 1, 7), ("r", 1, 1, 2, 7), ("m3", 1), ("r", 1, 2, 2, 7), ("r", 1, 2, 1, 7),
    ("al", 0, 1), ("r", 1, 2, 3, 7), ("r", 1, 2, 0, 7), ("m4", 1), ("m3", 2), ("m4", 2), ("m4", 3), ("al", 0, 2),
    ("m4", 0), ("m5", 1), ("en", 0, 1), ("al", 1, 1), ("m5", 2), ("en", 0, 2), ("m5", 3), ("al", 1, 2), ("m6", 0),
    ("m6", 1), ("al", 1, 3), ("m6", 3), ("m6", 2), ("en", 1, 1), ("en", 1, 2),
)


def place(turn, block):
    bits = [(block >> (3 - d)) & 1 for d in range(4)]
    index = 0
    for step in range(4):
        index = index * 2 + bits[(turn + step) % 4]
    return index


PLACES = [[place(j, i) for i in range(8)] for j in range(4)]


def at(turn, core, i):
    return PLACES[turn][i] if core == 0 else BLOCKS - 1 - PLACES[turn][i]


def kernel(
    x_hbm, wg_hbm, wu_hbm, wd_hbm, ct_hbm,
    out, ig, gg, ug, dg,
    x_in, ct_in, xs, cts, wg, wu, wd,
    p_gu, r_gu, d_all, o_part, o_sib, o_z, o_sum,
    p_h0, p_h1, p_h2, p_h3, r_h0, r_h1, r_h2, r_h3, h0, h1, h2, h3,
    load_sem, ssem, rsem, last_sem, zs_sem, zr_sem, ss_sem, sr_sem,
):
    p_hg, r_hg, h_all = (p_h0, p_h1, p_h2, p_h3), (r_h0, r_h1, r_h2, r_h3), (h0, h1, h2, h3)
    row, col = lax.axis_index("row"), lax.axis_index("col")
    y, x = row // 4, row % 4
    z, core = col // 2, col % 2
    partner = (
        (y * 4 + x + 1 - 2 * (x % 2), col),
        ((y + 1 - 2 * (y % 2)) * 4 + x, col),
        (y * 4 + 3 - x, col),
        ((3 - y) * 4 + x, col),
    )
    bits = (((x + 1) // 2) % 2, ((y + 1) // 2) % 2, x // 2, y // 2)
    mine = []
    for turn in range(4):
        index = 0
        for step in range(4):
            index = index * 2 + bits[(turn + step) % 4]
        mine.append(index)
    sibling = (row, z * 2 + 1 - core)
    along = {d: (row, lax.rem(z + d * (1 - 2 * core) + CHIPS, CHIPS) * 2 + core) for d in FAR}

    loads = []
    for i, (src, dst) in enumerate(
        ((x_hbm, x_in), (ct_hbm, ct_in), (wg_hbm, wg), (wu_hbm, wu), (wd_hbm, wd))
    ):
        loads.append(pltpu.make_async_copy(src, dst, load_sem.at[i]))
        loads[-1].start()

    barrier = pltpu.get_barrier_semaphore()
    peers = list(along.values()) + list(partner) + [sibling]
    for peer in peers:
        pl.semaphore_signal(barrier, inc=1, device_id=peer, device_id_type=MESH)
    loads[0].wait()
    loads[1].wait()
    pl.semaphore_wait(barrier, len(peers))

    def remote(src, dst, send_sem, recv_sem, device):
        return pltpu.make_async_remote_copy(
            src_ref=src, dst_ref=dst, send_sem=send_sem, recv_sem=recv_sem,
            device_id=device, device_id_type=MESH,
        )

    stores, sources = (xs, cts), (x_in, ct_in)
    first_done = set()

    def once(key, act):
        if key not in first_done:
            first_done.add(key)
            act()

    def region(kind, who, group):
        if group == 3:
            return stores[kind].at[who, pl.ds(0, OWN)]
        lo = OWN if group == 0 else group * HALF
        return stores[kind].at[who, pl.ds(lo, (group + 1) * HALF - lo)]

    def gather_start(kind, group):
        own = sources[kind]
        if group == 0:
            spot = region(kind, core, 3)
            remote(own, spot, ss_sem.at[kind, 3], sr_sem.at[kind, 3], sibling).start()
        for d, lo, count, first in runs(group):
            if d != 0:
                remote(
                    own.at[pl.ds(lo, count)], stores[kind].at[core, pl.ds(group * HALF + first, count)],
                    zs_sem.at[kind, group], zr_sem.at[kind, group], along[back(d)],
                ).start()
        if group == 0:
            spot[...] = own[...]

    def gather_share(kind, group):
        whole = region(kind, core, group)
        remote(whole, whole, zs_sem.at[kind, group], zr_sem.at[kind, group], sibling).wait_recv()
        remote(whole, whole, ss_sem.at[kind, group], sr_sem.at[kind, group], sibling).start()

    def gather_end(kind, group):
        def act():
            whole = region(kind, 1 - core, group)
            remote(whole, whole, ss_sem.at[kind, group], sr_sem.at[kind, group], sibling).wait_recv()
        once(("gathered", kind, group), act)

    def gather_sent(kind, group):
        whole = region(kind, core, group)
        if group < 3:
            remote(whole, whole, zs_sem.at[kind, group], zr_sem.at[kind, group], sibling).wait_send()
        remote(whole, whole, ss_sem.at[kind, group], sr_sem.at[kind, group], sibling).wait_send()

    def rows_of(buffer, c):
        return buffer[:, c * HALF:(c + 1) * HALF, :].reshape(2 * HALF, D)

    def turn_of(lane, j, step):
        return (j + 2) % 4 if lane == 1 and step < 4 else j

    def dim_of(lane, j, step):
        turn = turn_of(lane, j, step)
        return (turn + step) % 4 if step < 4 else (turn + 7 - step) % 4

    def ends(lane, c, j, step):
        own = mine[turn_of(lane, j, step)]
        if step < 4:
            part, arrive = (p_gu.at[c, j], r_gu.at[c, j]) if lane == 0 else (p_hg[j].at[c], r_hg[j].at[c])
            half = 8 >> step
            keep = own // half * half
            give = keep + half - 2 * half * (own // half % 2)
            return part.at[pl.ds(give, half)], arrive.at[pl.ds(BASE[step], half)]
        buffer = h_all[j].at[c] if lane == 0 else d_all.at[c, j]
        size = 1 << (step - 4)
        region = buffer.at[pl.ds(own // size * size, size)]
        return region, region

    SLOT = (0, 1, 2, 3, 2, 1, 0)

    def semaphores(lane, c, j, step):
        if lane == 0:
            leaving = ssem.at[0] if step < 4 else ssem.at[1 + j]
        else:
            leaving = ssem.at[5 + j] if step < 4 else ssem.at[9]
        coming = last_sem.at[lane * CHUNKS + c] if step == 7 else rsem.at[lane, c, turn_of(lane, j, step), SLOT[step]]
        return leaving, coming

    def copy_of(lane, c, j, step):
        return remote(
            *ends(lane, c, j, step), *semaphores(lane, c, j, step), partner[dim_of(lane, j, step)]
        )

    def launch(lane, c, j, step):
        if (lane, c, step) != (1, 2, 7):
            copy_of(lane, c, j, step).start()
            return
        high = mine[j] // 8
        for i in range(8):
            p = PLACES[j][i]
            block = d_all.at[c, j, pl.ds(p + (high if p < 8 else 1 - high) * (15 - 2 * p), 1)]
            leaving, coming = semaphores(lane, c, j, step)
            if i >= AHEAD:
                coming = last_sem.at[2 * CHUNKS]
            remote(block, block, leaving, coming, partner[dim_of(lane, j, step)]).start()

    def launch_blocks(lane, j, first, count):
        part, arrive = (p_gu.at[0, j], r_gu.at[0, j]) if lane == 0 else (p_hg[j].at[0], r_hg[j].at[0])
        turn = turn_of(lane, j, 0)
        high = mine[turn] // 8
        for i in range(first, first + count):
            p = PLACES[turn][i]
            q = p + (1 - high if p < 8 else high) * (15 - 2 * p)
            remote(
                part.at[pl.ds(q, 1)], arrive.at[pl.ds(q - 8 * (1 - high), 1)],
                *semaphores(lane, 0, j, 0), partner[dim_of(lane, j, 0)],
            ).start()

    def arrived(lane, c, j, step):
        if step < 4:
            copy_of(lane, c, j, step).wait_recv()
        else:
            own = mine[j]
            size = 1 << (step - 4)
            buffer = h_all[j].at[c] if lane == 0 else d_all.at[c, j]
            keep = own // size * size
            other = buffer.at[pl.ds(keep + size - 2 * size * (own // size % 2), size)]
            remote(
                other, other, *semaphores(lane, c, j, step), partner[dim_of(lane, j, step)]
            ).wait_recv()

    def add_arrived(lane, c, j, step, given):
        part, arrive = (p_gu.at[c, j], r_gu.at[c, j]) if lane == 0 else (p_hg[j].at[c], r_hg[j].at[c])
        index = mine[turn_of(lane, j, step)]
        half, wide = 8 >> step, 16 >> step
        start = index // wide * wide
        keep = index // half * half
        give = keep + half - 2 * half * (index // half % 2)

        first = give if given else keep

        def body(i, carry):
            where = first + i
            part[where] = (
                part[where].astype(jnp.float32) + arrive[BASE[step - 1] + where - start].astype(jnp.float32)
            ).astype(jnp.bfloat16)
            return carry

        lax.fori_loop(0, half, body, 0)

    def reduce_step(lane, c, j, step):
        arrived(lane, c, j, step - 1)
        add_arrived(lane, c, j, step, True)
        launch(lane, c, j, step)

    def reduce_rest(lane, c, j, step):
        add_arrived(lane, c, j, step, False)

    def total_of(lane, c, j):
        part, arrive = (p_gu.at[c, j], r_gu.at[c, j]) if lane == 0 else (p_hg[j].at[c], r_hg[j].at[c])
        return part[mine[turn_of(lane, j, 0)]].astype(jnp.float32) + arrive[BASE[3]].astype(jnp.float32)

    def store_partial(ref, turn, lo, value, first, count):
        width = value.shape[1]
        value = value.astype(jnp.bfloat16)
        for k in range(2 * count):
            ref[at(turn, k // count, first + k % count), :, lo:lo + width] = value[k * ROWS:(k + 1) * ROWS, :]

    def some_rows(buffer, c, first, count):
        lo = c * HALF + first * ROWS
        return buffer[:, lo:lo + count * ROWS, :].reshape(2 * count * ROWS, D)

    def gate_up_product(c, j, first, count):
        once("w_gate", loads[2].wait)
        once("w_up", loads[3].wait)
        value = some_rows(xs, c, first, count)
        ref, start = p_gu.at[c, j], 0
        for weight, (lo, width) in ((wg, SETS[j]), (wu, SETS[(j + 2) % 4])):
            term = jnp.dot(value, weight[:, lo:lo + width], preferred_element_type=jnp.float32)
            store_partial(ref, j, start, term, first, count)
            start += width

    def hidden_grad_product(c, j, first, count):
        once("w_down", loads[4].wait)
        lo, width = SETS[j]
        value = some_rows(cts, c, first, count)
        term = lax.dot_general(value, wd[lo:lo + width, :], contract_cols, preferred_element_type=jnp.float32)
        store_partial(p_hg[j].at[c], (j + 2) % 4, 0, term, first, count)

    def gate_up_early(j):
        gather_end(0, 3)
        gate_up_product(0, j, 0, EARLY)
        launch_blocks(0, j, 0, EARLY)

    def hidden_grad_early(j):
        gather_end(1, 3)
        hidden_grad_product(0, j, 0, EARLY)
        launch_blocks(1, j, 0, EARLY)

    def gate_up(c, j):
        gather_end(0, c)
        if c == 0:
            gate_up_product(0, j, EARLY, 8 - EARLY)
            launch_blocks(0, j, EARLY, 8 - EARLY)
        else:
            gate_up_product(c, j, 0, 8)
            launch(0, c, j, 0)

    def hidden_grad(c, j):
        gather_end(1, c)
        if c == 0:
            hidden_grad_product(0, j, EARLY, 8 - EARLY)
            launch_blocks(1, j, EARLY, 8 - EARLY)
        else:
            hidden_grad_product(c, j, 0, 8)
            launch(1, c, j, 0)

    def make_hidden(c, pair):
        streams = (pair, pair + 2)
        for j in streams:
            arrived(0, c, j, 3)
        sums = {j: total_of(0, c, j) for j in streams}
        for j in streams:
            width = SETS[j][1]
            gate = sums[j][:, :width]
            up = sums[(j + 2) % 4][:, WIDE - width:]
            h_all[j][c, mine[j]] = (gate * jax.nn.sigmoid(gate) * up).astype(jnp.bfloat16)
            launch(0, c, j, 4)

    def make_deltas(c, pair):
        streams = (pair, pair + 2)
        for j in streams:
            arrived(1, c, j, 3)
        sums = {j: total_of(0, c, j) for j in streams}
        for j in streams:
            other = (j + 2) % 4
            width = SETS[j][1]
            gate = sums[j][:, :width]
            up = sums[other][:, WIDE - width:]
            grad = total_of(1, c, j)
            s = jax.nn.sigmoid(gate)
            d_all[c, j, mine[j], :, :width] = (grad * up * s * (1.0 + gate * (1.0 - s))).astype(jnp.bfloat16)
            d_all[c, other, mine[other], :, WIDE - width:] = (grad * gate * s).astype(jnp.bfloat16)
        for j in streams:
            launch(1, c, j, 4)

    def tokens(ref, c, j, lo, width, first=0, count=8):
        blocks = [ref[c, at(j, k // count, first + k % count), :, lo:lo + width] for k in range(2 * count)]
        return jnp.concatenate(blocks, axis=0)

    def hidden_of(c, j):
        return tokens(h_all[j], c, j, 0, SETS[j][1])

    def gate_delta_of(c, j, *some):
        return tokens(d_all.at[:, j], c, j, 0, SETS[j][1], *some)

    def up_delta_of(c, j, *some):
        other = (j + 2) % 4
        return tokens(d_all.at[:, other], c, other, WIDE - SETS[j][1], SETS[j][1], *some)

    def gathered(lane, c, ahead=False):
        def act(size, sem):
            remote(size, size, ssem.at[1], last_sem.at[sem], sibling).wait_recv()

        split = (lane, c) == (1, 2)
        if lane == 0:
            size = p_gu.at[c, 0]
        else:
            size = d_all.at[c, :, pl.ds(0, AHEAD if split else 8)]
        once(("doubled", lane, c), lambda: act(size, lane * CHUNKS + c))
        if split and not ahead:
            once("rest", lambda: act(d_all.at[c, :, pl.ds(0, 8 - AHEAD)], 2 * CHUNKS))

    def share_of(kind, c, first, count):
        rows = pl.ds(first * ROWS, count * ROWS)
        slot = c if first == 0 else 3
        return remote(
            o_part.at[kind, c, 1 - core, rows], o_sib.at[kind, c, rows],
            ss_sem.at[kind, slot], sr_sem.at[2 + kind, slot], sibling,
        )

    def scatter_start(kind, c, total, first=0, count=8):
        rows = count * ROWS
        o_part[kind, c, :, first * ROWS:first * ROWS + rows, :] = total.astype(jnp.bfloat16).reshape(2, rows, D)
        once(("sent", kind, c, first), lambda: gather_sent(kind, c if first == 0 else 3))
        share_of(kind, c, first, count).start()

    def scatter_along(kind, c, first=0, count=8):
        share_of(kind, c, first, count).wait_recv()
        lo, hi = first * ROWS, (first + count) * ROWS
        o_part[kind, c, core, lo:hi, :] = (
            o_part[kind, c, core, lo:hi, :].astype(jnp.float32) + o_sib[kind, c, lo:hi, :].astype(jnp.float32)
        ).astype(jnp.bfloat16)
        for d, row, rows, start in runs(c, first, count):
            if d != 0:
                remote(
                    o_part.at[kind, c, core, pl.ds(start, rows)],
                    o_z.at[kind, pl.ds(FAR.index(back(d)) * OWN + row, rows)],
                    zs_sem.at[kind, c], zr_sem.at[2 + kind, c], along[d],
                ).start()

    def landed(kind, c):
        whole = o_z.at[kind, pl.ds(0, HALF - (OWN if c == 0 else 0))]
        return remote(whole, whole, zs_sem.at[kind, c], zr_sem.at[2 + kind, c], sibling)

    def scatter_end(kind, c):
        landed(kind, c).wait_recv()
        for d, row, rows, start in runs(c):
            if d == 0:
                o_sum[kind] = o_part[kind, c, core, 0:OWN, :].astype(jnp.float32)
            else:
                spot = FAR.index(back(d)) * OWN + row
                o_sum[kind, row:row + rows, :] += o_z[kind, spot:spot + rows, :].astype(jnp.float32)
        if c == CHUNKS - 1:
            (out, ig)[kind][...] = o_sum[kind].astype(jnp.bfloat16)

    def output_part(c):
        gathered(0, c)
        total = None
        for j in range(4):
            lo, width = SETS[j]
            term = jnp.dot(hidden_of(c, j), wd[lo:lo + width, :], preferred_element_type=jnp.float32)
            total = term if total is None else total + term
        scatter_start(0, c, total)

    def input_grad_part(c):
        split = c >= CHUNKS - 1
        some = (((0, AHEAD), (AHEAD, 8 - AHEAD))[c - 2]) if split else (0, 8)
        gathered(1, min(c, 2), c == 2)
        total = None
        for j in range(4):
            lo, width = SETS[j]
            term = lax.dot_general(
                gate_delta_of(min(c, 2), j, *some), wg[:, lo:lo + width], contract_cols,
                preferred_element_type=jnp.float32,
            ) + lax.dot_general(
                up_delta_of(min(c, 2), j, *some), wu[:, lo:lo + width], contract_cols,
                preferred_element_type=jnp.float32,
            )
            total = term if total is None else total + term
        scatter_start(1, min(c, 2), total, *some)

    def along_part(kind, c):
        if kind == 1 and c >= CHUNKS - 1:
            scatter_along(1, 2, *((0, AHEAD), (AHEAD, 8 - AHEAD))[c - 2])
        else:
            scatter_along(kind, c)

    def over_tokens(left, right):
        a = jnp.concatenate([left(c) for c in range(CHUNKS)], axis=0)
        b = jnp.concatenate([right(c) for c in range(CHUNKS)], axis=0)
        return lax.dot_general(a, b, contract_rows, preferred_element_type=jnp.float32).astype(jnp.bfloat16)

    def down_grad(j):
        for c in range(CHUNKS):
            gathered(0, c)
        lo, width = SETS[j]
        dg[lo:lo + width, :] = over_tokens(lambda c: hidden_of(c, j), lambda c: rows_of(cts, c))

    def input_side_grads(j):
        for c in range(CHUNKS):
            gathered(1, c)
        lo, width = SETS[j]
        for res, of in ((gg, gate_delta_of), (ug, up_delta_of)):
            res[:, lo:lo + width] = over_tokens(lambda c: rows_of(xs, c), lambda c: of(c, j))

    def halve_or_double(lane, c, j, step):
        if step < 4:
            reduce_step(lane, c, j, step)
        else:
            arrived(lane, c, j, step - 1)
            launch(lane, c, j, step)

    acts = {
        "x": lambda c: gather_start(0, c), "c": lambda c: gather_start(1, c),
        "sx": lambda c: gather_share(0, c), "sc": lambda c: gather_share(1, c),
        "gu": gate_up, "hg": hidden_grad, "r": halve_or_double, "k": reduce_rest, "mh": make_hidden, "md": make_deltas,
        "m3": output_part, "m5": input_grad_part, "al": along_part, "ga": gate_up_early, "ha": hidden_grad_early, "en": scatter_end,
        "m4": down_grad, "m6": input_side_grads,
    }
    for act, *where in ORDER:
        acts[act](*where)

    left = [(r_gu, 0)]
    for j in range(4):
        left += [(h_all[j].at[:, pl.ds(0, BLOCKS - 1)], 1 + j), (r_hg[j], 5 + j)]
    left.append((d_all.at[:, :, pl.ds(0, BLOCKS - 1)], 9))
    for size, i in left:
        remote(size, size, ssem.at[i], last_sem.at[0], sibling).wait_send()
    gather_sent(0, 3)
    for kind in range(2):
        for c in range(CHUNKS):
            landed(kind, c).wait_send()
            if (kind, c) == (1, 2):
                share_of(1, 2, 0, AHEAD).wait_send()
                share_of(1, 2, AHEAD, 8 - AHEAD).wait_send()
            else:
                share_of(kind, c, 0, 8).wait_send()


def deliver(*refs):
    sources, results, sem = refs[:5], refs[5:10], refs[10]
    copies = []
    for src, dst in zip(sources, results):
        parts = 1 if src.shape[0] == OWN else PARTS
        step = src.shape[0] // parts
        for lo in range(0, src.shape[0], step):
            rows = pl.ds(lo, step)
            copies.append(pltpu.make_async_copy(src.at[rows], dst.at[rows], sem.at[len(copies)]))
    for copy in copies:
        copy.start()
    for copy in copies:
        copy.wait()


def local(inputs, w_gate, w_up, w_down, cotangent):
    bf16, f32 = jnp.bfloat16, jnp.float32
    vmem = pltpu.VMEM
    scratch = [
        vmem((OWN, D), bf16),
        vmem((OWN, D), bf16),
        vmem((2, CHUNKS * HALF, D), bf16),
        vmem((2, CHUNKS * HALF, D), bf16),
        vmem((D, F), bf16),
        vmem((D, F), bf16),
        vmem((F, D), bf16),
        vmem((CHUNKS, 4, BLOCKS, ROWS, WIDE), bf16),
        vmem((CHUNKS, 4, BLOCKS - 1, ROWS, WIDE), bf16),
        vmem((CHUNKS, 4, BLOCKS, ROWS, WIDE), bf16),
        vmem((2, CHUNKS, 2, HALF, D), bf16),
        vmem((2, CHUNKS, HALF, D), bf16),
        vmem((2, len(FAR) * OWN, D), bf16),
        vmem((2, OWN, D), f32),
    ]
    for count in (BLOCKS, BLOCKS - 1, BLOCKS):
        scratch += [vmem((CHUNKS, count, ROWS, width), bf16) for _, width in SETS]
    dma = pltpu.SemaphoreType.DMA
    scratch += [
        dma((5,)), dma((10,)), dma((2, CHUNKS, 4, 4)), dma((2 * CHUNKS + 1,)),
        dma((2, CHUNKS)), dma((4, CHUNKS)), dma((2, 4)), dma((4, 4)),
    ]
    whole = pl.BlockSpec(memory_space=pltpu.HBM)
    here = pl.BlockSpec(memory_space=pltpu.VMEM)
    results = (inputs, inputs, w_gate, w_up, w_down)
    held = pl.pallas_call(
        kernel,
        out_shape=tuple(pltpu.VMEM(a.shape, bf16) for a in results),
        in_specs=[whole] * 5,
        out_specs=[here] * 5,
        scratch_shapes=scratch,
        compiler_params=pltpu.CompilerParams(
            collective_id=0, has_side_effects=True, vmem_limit_bytes=40 * 2**20
        ),
    )(*[pltpu.with_memory_space_constraint(a, pltpu.HBM) for a in (inputs, w_gate, w_up, w_down, cotangent)])
    held = [pltpu.with_memory_space_constraint(a, pltpu.VMEM) for a in held]
    return pl.pallas_call(
        deliver,
        out_shape=tuple(jax.ShapeDtypeStruct(a.shape, bf16) for a in results),
        in_specs=[here] * 5,
        out_specs=[whole] * 5,
        scratch_shapes=[dma((2 + 3 * PARTS,))],
        compiler_params=pltpu.CompilerParams(vmem_limit_bytes=2**20),
    )(*held)


def solution(mesh):
    return jax.shard_map(
        local,
        mesh=mesh,
        in_specs=(P("col", "row"), P("row", "col"), P("row", "col"), P("col", "row"), P("col", "row")),
        out_specs=(P("col", "row"), P("col", "row"), P("row", "col"), P("row", "col"), P("col", "row")),
        check_vma=False,
    )
```

```python
import jax
import jax.numpy as jnp
from jax import lax
from jax.experimental import pallas as pl
from jax.experimental.pallas import tpu as pltpu
from jax.sharding import PartitionSpec as P

MESH = pl.DeviceIdType.MESH
ROWS = 16
OWN = 48
CHUNKS = 3
BLOCKS = 16
CHIPS = 8
SETS = ((0, 512), (512, 512), (1024, 384), (1408, 384))
D, F = 512, 1792
WIDE = 896
HALF = 128
PARTS = 1
BASE = (0, 8, 12, 14)

LAYOUT = (
    ((0, 0), (0, 1), (0, 2), (1, 0), (1, 1), (1, 2), (-1, 0), (-1, 1)),
    ((3, 1), (3, 2), (4, 0), (4, 1), (4, 2), (-3, 0), (-3, 1), (-3, 2)),
    ((3, 0), (2, 0), (2, 1), (-2, 0), (-2, 1), (2, 2), (-2, 2), (-1, 2)),
)
FAR = (1, -1, 2, -2, 3, 4, -3)
EARLY = 3
AHEAD = 5


def runs(c, first=0, count=8):
    found = []
    for i in range(first, first + count):
        d, part = LAYOUT[c][i]
        if found and found[-1][0] == d and found[-1][1] + found[-1][2] == part * ROWS:
            found[-1][2] += ROWS
        else:
            found.append([d, part * ROWS, ROWS, i * ROWS])
    return found


def back(d):
    return d if d == 4 else -d


contract_rows = (((0,), (0,)), ((), ()))
contract_cols = (((1,), (1,)), ((), ()))

ORDER = (
    ("x", 0), ("c", 0), ("ga", 0), ("ha", 0), ("ha", 2), ("ha", 3), ("ga", 3), ("ha", 1), ("ga", 2), ("ga", 1),
    ("sx", 0), ("x", 1), ("x", 2), ("sc", 0), ("c", 1), ("c", 2), ("gu", 0, 2), ("gu", 0, 3), ("gu", 0, 1), ("hg",
    0, 3), ("hg", 0, 1), ("gu", 0, 0), ("hg", 0, 0), ("hg", 0, 2), ("r", 0, 0, 2, 1), ("k", 0, 0, 2, 1), ("r", 0, 0,
    3, 1), ("k", 0, 0, 3, 1), ("r", 0, 0, 1, 1), ("k", 0, 0, 1, 1), ("sx", 1), ("r", 0, 0, 0, 1), ("k", 0, 0, 0, 1),
    ("r", 1, 0, 0, 1), ("k", 1, 0, 0, 1), ("r", 1, 0, 3, 1), ("k", 1, 0, 3, 1), ("r", 1, 0, 1, 1), ("k", 1, 0, 1,
    1), ("gu", 1, 0), ("r", 1, 0, 2, 1), ("k", 1, 0, 2, 1), ("gu", 1, 3), ("gu", 1, 2), ("gu", 1, 1), ("sx", 2),
    ("gu", 2, 3), ("r", 0, 0, 2, 2), ("r", 0, 0, 3, 2), ("k", 0, 0, 3, 2), ("k", 0, 0, 2, 2), ("gu", 2, 2), ("r", 0,
    0, 1, 2), ("k", 0, 0, 1, 2), ("gu", 2, 0), ("r", 1, 0, 0, 2), ("r", 0, 0, 0, 2), ("k", 1, 0, 0, 2), ("k", 0, 0,
    0, 2), ("gu", 2, 1), ("r", 1, 0, 3, 2), ("r", 1, 0, 1, 2), ("k", 1, 0, 3, 2), ("k", 1, 0, 1, 2), ("r", 1, 0, 2,
    2), ("k", 1, 0, 2, 2), ("sc", 1), ("hg", 1, 1), ("hg", 1, 0), ("hg", 1, 2), ("hg", 1, 3), ("sc", 2), ("r", 0, 1,
    3, 1), ("k", 0, 1, 3, 1), ("r", 0, 1, 2, 1), ("k", 0, 1, 2, 1), ("r", 0, 1, 0, 1), ("k", 0, 1, 0, 1), ("hg", 2,
    3), ("hg", 2, 1), ("r", 0, 1, 1, 1), ("k", 0, 1, 1, 1), ("hg", 2, 0), ("r", 0, 0, 2, 3), ("k", 0, 0, 2, 3),
    ("hg", 2, 2), ("r", 0, 0, 3, 3), ("k", 0, 0, 3, 3), ("r", 0, 2, 3, 1), ("k", 0, 2, 3, 1), ("r", 0, 2, 2, 1),
    ("k", 0, 2, 2, 1), ("r", 0, 0, 1, 3), ("k", 0, 0, 1, 3), ("r", 0, 0, 0, 3), ("k", 0, 0, 0, 3), ("r", 0, 2, 0,
    1), ("k", 0, 2, 0, 1), ("r", 1, 0, 3, 3), ("k", 1, 0, 3, 3), ("r", 1, 0, 2, 3), ("k", 1, 0, 2, 3), ("r", 1, 0,
    0, 3), ("k", 1, 0, 0, 3), ("r", 0, 2, 1, 1), ("k", 0, 2, 1, 1), ("r", 1, 0, 1, 3), ("k", 1, 0, 1, 3), ("r", 1,
    1, 2, 1), ("k", 1, 1, 2, 1), ("r", 1, 1, 1, 1), ("k", 1, 1, 1, 1), ("r", 1, 1, 0, 1), ("k", 1, 1, 0, 1), ("r",
    1, 1, 3, 1), ("k", 1, 1, 3, 1), ("r", 0, 1, 3, 2), ("k", 0, 1, 3, 2), ("r", 0, 1, 2, 2), ("k", 0, 1, 2, 2),
    ("r", 0, 1, 1, 2), ("k", 0, 1, 1, 2), ("r", 0, 1, 0, 2), ("k", 0, 1, 0, 2), ("r", 1, 2, 2, 1), ("k", 1, 2, 2,
    1), ("r", 1, 2, 3, 1), ("k", 1, 2, 3, 1), ("r", 1, 2, 1, 1), ("k", 1, 2, 1, 1), ("r", 1, 2, 0, 1), ("k", 1, 2,
    0, 1), ("r", 0, 2, 3, 2), ("k", 0, 2, 3, 2), ("mh", 0, 1), ("r", 0, 2, 2, 2), ("k", 0, 2, 2, 2), ("r", 0, 2, 0,
    2), ("k", 0, 2, 0, 2), ("mh", 0, 0), ("md", 0, 0), ("r", 0, 2, 1, 2), ("k", 0, 2, 1, 2), ("md", 0, 1), ("r", 1,
    1, 1, 2), ("k", 1, 1, 1, 2), ("r", 1, 1, 2, 2), ("k", 1, 1, 2, 2), ("r", 1, 1, 0, 2), ("k", 1, 1, 0, 2), ("r",
    1, 1, 3, 2), ("k", 1, 1, 3, 2), ("r", 0, 1, 2, 3), ("k", 0, 1, 2, 3), ("r", 0, 1, 3, 3), ("k", 0, 1, 3, 3),
    ("r", 0, 1, 1, 3), ("k", 0, 1, 1, 3), ("r", 0, 1, 0, 3), ("k", 0, 1, 0, 3), ("r", 1, 2, 1, 2), ("k", 1, 2, 1,
    2), ("r", 1, 2, 2, 2), ("k", 1, 2, 2, 2), ("r", 0, 0, 1, 5), ("r", 1, 2, 3, 2), ("k", 1, 2, 3, 2), ("r", 0, 0,
    3, 5), ("r", 1, 2, 0, 2), ("k", 1, 2, 0, 2), ("r", 0, 0, 0, 5), ("r", 0, 2, 3, 3), ("k", 0, 2, 3, 3), ("r", 0,
    2, 2, 3), ("k", 0, 2, 2, 3), ("r", 0, 0, 2, 5), ("r", 1, 0, 0, 5), ("r", 0, 2, 0, 3), ("k", 0, 2, 0, 3), ("r",
    1, 0, 1, 5), ("r", 1, 0, 2, 5), ("r", 1, 0, 3, 5), ("r", 1, 1, 0, 3), ("k", 1, 1, 0, 3), ("r", 1, 1, 1, 3),
    ("r", 0, 2, 1, 3), ("k", 1, 1, 1, 3), ("k", 0, 2, 1, 3), ("r", 1, 1, 2, 3), ("k", 1, 1, 2, 3), ("r", 1, 1, 3,
    3), ("k", 1, 1, 3, 3), ("mh", 1, 1), ("mh", 1, 0), ("r", 1, 2, 2, 3), ("k", 1, 2, 2, 3), ("r", 1, 2, 1, 3),
    ("k", 1, 2, 1, 3), ("r", 1, 2, 0, 3), ("k", 1, 2, 0, 3), ("r", 0, 0, 3, 6), ("r", 0, 0, 1, 6), ("r", 0, 0, 0,
    6), ("r", 1, 2, 3, 3), ("r", 0, 0, 2, 6), ("k", 1, 2, 3, 3), ("mh", 2, 0), ("r", 1, 0, 2, 6), ("r", 1, 0, 0, 6),
    ("r", 1, 0, 3, 6), ("r", 1, 0, 1, 6), ("mh", 2, 1), ("r", 0, 1, 3, 5), ("md", 1, 0), ("r", 0, 1, 2, 5), ("md",
    1, 1), ("r", 0, 1, 0, 5), ("r", 0, 1, 1, 5), ("md", 2, 0), ("r", 0, 0, 3, 7), ("md", 2, 1), ("r", 0, 0, 1, 7),
    ("r", 0, 0, 2, 7), ("r", 0, 0, 0, 7), ("r", 0, 2, 2, 5), ("r", 0, 2, 0, 5), ("r", 1, 0, 2, 7), ("r", 1, 0, 0,
    7), ("r", 1, 0, 3, 7), ("r", 1, 0, 1, 7), ("r", 0, 2, 1, 5), ("r", 0, 1, 3, 6), ("r", 1, 1, 0, 5), ("r", 0, 2,
    3, 5), ("r", 0, 1, 2, 6), ("r", 1, 1, 2, 5), ("r", 1, 1, 3, 5), ("r", 0, 1, 1, 6), ("r", 1, 1, 1, 5), ("r", 1,
    2, 2, 5), ("r", 1, 2, 0, 5), ("r", 0, 1, 0, 6), ("r", 1, 2, 1, 5), ("r", 1, 2, 3, 5), ("m3", 0), ("r", 0, 2, 0,
    6), ("r", 0, 2, 2, 6), ("al", 0, 0), ("r", 0, 2, 1, 6), ("r", 0, 2, 3, 6), ("m5", 0), ("r", 1, 1, 0, 6), ("r",
    1, 1, 3, 6), ("r", 1, 1, 1, 6), ("r", 0, 1, 2, 7), ("r", 0, 1, 3, 7), ("en", 0, 0), ("r", 0, 1, 0, 7), ("r", 1,
    1, 2, 6), ("r", 0, 1, 1, 7), ("r", 1, 2, 1, 6), ("al", 1, 0), ("r", 1, 2, 3, 6), ("r", 1, 2, 2, 6), ("r", 1, 2,
    0, 6), ("r", 0, 2, 2, 7), ("r", 0, 2, 3, 7), ("r", 0, 2, 0, 7), ("r", 0, 2, 1, 7), ("en", 1, 0), ("r", 1, 1, 3,
    7), ("r", 1, 1, 0, 7), ("r", 1, 1, 1, 7), ("r", 1, 1, 2, 7), ("m3", 1), ("r", 1, 2, 2, 7), ("r", 1, 2, 1, 7),
    ("al", 0, 1), ("r", 1, 2, 3, 7), ("r", 1, 2, 0, 7), ("m4", 1), ("m3", 2), ("m4", 2), ("m4", 3), ("al", 0, 2),
    ("m4", 0), ("m5", 1), ("en", 0, 1), ("al", 1, 1), ("m5", 2), ("en", 0, 2), ("m5", 3), ("al", 1, 2), ("m6", 0),
    ("m6", 1), ("al", 1, 3), ("m6", 3), ("m6", 2), ("en", 1, 1), ("en", 1, 2),
)


def place(turn, block):
    bits = [(block >> (3 - d)) & 1 for d in range(4)]
    index = 0
    for step in range(4):
        index = index * 2 + bits[(turn + step) % 4]
    return index


PLACES = [[place(j, i) for i in range(8)] for j in range(4)]


def at(turn, core, i):
    return PLACES[turn][i] if core == 0 else BLOCKS - 1 - PLACES[turn][i]


def kernel(
    x_hbm, wg_hbm, wu_hbm, wd_hbm, ct_hbm,
    out, ig, gg, ug, dg,
    x_in, ct_in, xs, cts, wg, wu, wd,
    p_gu, r_gu, d_all, o_part, o_sib, o_z, o_sum,
    p_h0, p_h1, p_h2, p_h3, r_h0, r_h1, r_h2, r_h3, h0, h1, h2, h3,
    load_sem, ssem, rsem, pair_sem, last_sem, zs_sem, zr_sem, ss_sem, sr_sem,
):
    p_hg, r_hg, h_all = (p_h0, p_h1, p_h2, p_h3), (r_h0, r_h1, r_h2, r_h3), (h0, h1, h2, h3)
    row, col = lax.axis_index("row"), lax.axis_index("col")
    y, x = row // 4, row % 4
    z, core = col // 2, col % 2
    partner = (
        (y * 4 + x + 1 - 2 * (x % 2), col),
        ((y + 1 - 2 * (y % 2)) * 4 + x, col),
        (y * 4 + 3 - x, col),
        ((3 - y) * 4 + x, col),
    )
    bits = (((x + 1) // 2) % 2, ((y + 1) // 2) % 2, x // 2, y // 2)
    mine = []
    for turn in range(4):
        index = 0
        for step in range(4):
            index = index * 2 + bits[(turn + step) % 4]
        mine.append(index)
    sibling = (row, z * 2 + 1 - core)
    along = {d: (row, lax.rem(z + d * (1 - 2 * core) + CHIPS, CHIPS) * 2 + core) for d in FAR}

    barrier = pltpu.get_barrier_semaphore()
    peers = [along[d] for d in (4, 3, -3, 2, -2, 1, -1)] + list(partner) + [sibling]
    for peer in peers:
        pl.semaphore_signal(barrier, inc=1, device_id=peer, device_id_type=MESH)
    loads = []
    for i, (src, dst) in enumerate(
        ((x_hbm, x_in), (ct_hbm, ct_in), (wg_hbm, wg), (wu_hbm, wu), (wd_hbm, wd))
    ):
        loads.append(pltpu.make_async_copy(src, dst, load_sem.at[i]))
        loads[-1].start()

    loads[0].wait()
    loads[1].wait()
    pl.semaphore_wait(barrier, len(peers))

    def remote(src, dst, send_sem, recv_sem, device):
        return pltpu.make_async_remote_copy(
            src_ref=src, dst_ref=dst, send_sem=send_sem, recv_sem=recv_sem,
            device_id=device, device_id_type=MESH,
        )

    stores, sources = (xs, cts), (x_in, ct_in)
    first_done = set()

    def once(key, act):
        if key not in first_done:
            first_done.add(key)
            act()

    def region(kind, who, group):
        if group == 3:
            return stores[kind].at[who, pl.ds(0, OWN)]
        lo = OWN if group == 0 else group * HALF
        return stores[kind].at[who, pl.ds(lo, (group + 1) * HALF - lo)]

    def gather_start(kind, group):
        own = sources[kind]
        if group == 0:
            spot = region(kind, core, 3)
            remote(own, spot, ss_sem.at[kind, 3], sr_sem.at[kind, 3], sibling).start()
        for d, lo, count, first in runs(group):
            if d != 0:
                remote(
                    own.at[pl.ds(lo, count)], stores[kind].at[core, pl.ds(group * HALF + first, count)],
                    zs_sem.at[kind, group], zr_sem.at[kind, group], along[back(d)],
                ).start()
        if group == 0:
            spot[...] = own[...]

    def gather_share(kind, group):
        whole = region(kind, core, group)
        remote(whole, whole, zs_sem.at[kind, group], zr_sem.at[kind, group], sibling).wait_recv()
        remote(whole, whole, ss_sem.at[kind, group], sr_sem.at[kind, group], sibling).start()

    def gather_end(kind, group):
        def act():
            whole = region(kind, 1 - core, group)
            remote(whole, whole, ss_sem.at[kind, group], sr_sem.at[kind, group], sibling).wait_recv()
        once(("gathered", kind, group), act)

    def gather_sent(kind, group):
        whole = region(kind, core, group)
        if group < 3:
            remote(whole, whole, zs_sem.at[kind, group], zr_sem.at[kind, group], sibling).wait_send()
        remote(whole, whole, ss_sem.at[kind, group], sr_sem.at[kind, group], sibling).wait_send()

    def rows_of(buffer, c):
        return buffer[:, c * HALF:(c + 1) * HALF, :].reshape(2 * HALF, D)

    def turn_of(lane, j, step):
        return (j + 2) % 4 if lane == 1 and step < 4 else j

    def dim_of(lane, j, step):
        turn = turn_of(lane, j, step)
        return (turn + step) % 4 if step < 4 else (turn + 7 - step) % 4

    def ends(lane, c, j, step):
        own = mine[turn_of(lane, j, step)]
        if step < 4:
            part, arrive = (p_gu.at[c, j], r_gu.at[c, j]) if lane == 0 else (p_hg[j].at[c], r_hg[j].at[c])
            half = 8 >> step
            keep = own // half * half
            give = keep + half - 2 * half * (own // half % 2)
            return part.at[pl.ds(give, half)], arrive.at[pl.ds(BASE[step], half)]
        buffer = h_all[j].at[c] if lane == 0 else d_all.at[c, j]
        size = 1 << (step - 4)
        region = buffer.at[pl.ds(own // size * size, size)]
        return region, region

    SLOT = (0, 1, 2, None, 2, 1, 0)

    def semaphores(lane, c, j, step):
        if lane == 0:
            leaving = ssem.at[0] if step < 4 else ssem.at[1 + j]
        else:
            leaving = ssem.at[5 + j] if step < 4 else ssem.at[9]
        if step == 7:
            coming = last_sem.at[lane * CHUNKS + c]
        elif step == 3:
            coming = pair_sem.at[lane, c, j % 2]
        else:
            coming = rsem.at[lane, c, turn_of(lane, j, step), SLOT[step]]
        return leaving, coming

    def copy_of(lane, c, j, step):
        return remote(
            *ends(lane, c, j, step), *semaphores(lane, c, j, step), partner[dim_of(lane, j, step)]
        )

    def launch(lane, c, j, step):
        if (lane, c, step) != (1, 2, 7):
            copy_of(lane, c, j, step).start()
            return
        high = mine[j] // 8
        for i in range(8):
            p = PLACES[j][i]
            block = d_all.at[c, j, pl.ds(p + (high if p < 8 else 1 - high) * (15 - 2 * p), 1)]
            leaving, coming = semaphores(lane, c, j, step)
            if i >= AHEAD:
                coming = last_sem.at[2 * CHUNKS]
            remote(block, block, leaving, coming, partner[dim_of(lane, j, step)]).start()

    def launch_blocks(lane, j, first, count):
        part, arrive = (p_gu.at[0, j], r_gu.at[0, j]) if lane == 0 else (p_hg[j].at[0], r_hg[j].at[0])
        turn = turn_of(lane, j, 0)
        high = mine[turn] // 8
        for i in range(first, first + count):
            p = PLACES[turn][i]
            q = p + (1 - high if p < 8 else high) * (15 - 2 * p)
            remote(
                part.at[pl.ds(q, 1)], arrive.at[pl.ds(q - 8 * (1 - high), 1)],
                *semaphores(lane, 0, j, 0), partner[dim_of(lane, j, 0)],
            ).start()

    def arrived(lane, c, j, step):
        if step < 4:
            copy_of(lane, c, j, step).wait_recv()
        else:
            own = mine[j]
            size = 1 << (step - 4)
            buffer = h_all[j].at[c] if lane == 0 else d_all.at[c, j]
            keep = own // size * size
            other = buffer.at[pl.ds(keep + size - 2 * size * (own // size % 2), size)]
            remote(
                other, other, *semaphores(lane, c, j, step), partner[dim_of(lane, j, step)]
            ).wait_recv()

    def add_arrived(lane, c, j, step, given):
        part, arrive = (p_gu.at[c, j], r_gu.at[c, j]) if lane == 0 else (p_hg[j].at[c], r_hg[j].at[c])
        index = mine[turn_of(lane, j, step)]
        half, wide = 8 >> step, 16 >> step
        start = index // wide * wide
        keep = index // half * half
        give = keep + half - 2 * half * (index // half % 2)

        first = give if given else keep

        def body(i, carry):
            where = first + i
            part[where] = (
                part[where].astype(jnp.float32) + arrive[BASE[step - 1] + where - start].astype(jnp.float32)
            ).astype(jnp.bfloat16)
            return carry

        lax.fori_loop(0, half, body, 0)

    def reduce_step(lane, c, j, step):
        arrived(lane, c, j, step - 1)
        add_arrived(lane, c, j, step, True)
        launch(lane, c, j, step)

    def reduce_rest(lane, c, j, step):
        add_arrived(lane, c, j, step, False)

    def total_of(lane, c, j):
        part, arrive = (p_gu.at[c, j], r_gu.at[c, j]) if lane == 0 else (p_hg[j].at[c], r_hg[j].at[c])
        return part[mine[turn_of(lane, j, 0)]].astype(jnp.float32) + arrive[BASE[3]].astype(jnp.float32)

    def store_partial(ref, turn, lo, value, first, count):
        width = value.shape[1]
        value = value.astype(jnp.bfloat16)
        for k in range(2 * count):
            ref[at(turn, k // count, first + k % count), :, lo:lo + width] = value[k * ROWS:(k + 1) * ROWS, :]

    def some_rows(buffer, c, first, count):
        lo = c * HALF + first * ROWS
        return buffer[:, lo:lo + count * ROWS, :].reshape(2 * count * ROWS, D)

    def gate_up_product(c, j, first, count):
        once("w_gate", loads[2].wait)
        once("w_up", loads[3].wait)
        value = some_rows(xs, c, first, count)
        ref, start = p_gu.at[c, j], 0
        for weight, (lo, width) in ((wg, SETS[j]), (wu, SETS[(j + 2) % 4])):
            term = jnp.dot(value, weight[:, lo:lo + width], preferred_element_type=jnp.float32)
            store_partial(ref, j, start, term, first, count)
            start += width

    def hidden_grad_product(c, j, first, count):
        once("w_down", loads[4].wait)
        lo, width = SETS[j]
        value = some_rows(cts, c, first, count)
        term = lax.dot_general(value, wd[lo:lo + width, :], contract_cols, preferred_element_type=jnp.float32)
        store_partial(p_hg[j].at[c], (j + 2) % 4, 0, term, first, count)

    def gate_up_early(j):
        gather_end(0, 3)
        gate_up_product(0, j, 0, EARLY)
        launch_blocks(0, j, 0, EARLY)

    def hidden_grad_early(j):
        gather_end(1, 3)
        hidden_grad_product(0, j, 0, EARLY)
        launch_blocks(1, j, 0, EARLY)

    def gate_up(c, j):
        gather_end(0, c)
        if c == 0:
            gate_up_product(0, j, EARLY, 8 - EARLY)
            launch_blocks(0, j, EARLY, 8 - EARLY)
        else:
            gate_up_product(c, j, 0, 8)
            launch(0, c, j, 0)

    def hidden_grad(c, j):
        gather_end(1, c)
        if c == 0:
            hidden_grad_product(0, j, EARLY, 8 - EARLY)
            launch_blocks(1, j, EARLY, 8 - EARLY)
        else:
            hidden_grad_product(c, j, 0, 8)
            launch(1, c, j, 0)

    def pair_arrived(lane, c, pair):
        size = r_gu.at[c, 0, pl.ds(0, 2 - lane)]
        remote(size, size, ssem.at[0], pair_sem.at[lane, c, pair], sibling).wait_recv()

    def make_hidden(c, pair):
        streams = (pair, pair + 2)
        pair_arrived(0, c, pair)
        sums = {j: total_of(0, c, j) for j in streams}
        for j in streams:
            width = SETS[j][1]
            gate = sums[j][:, :width]
            up = sums[(j + 2) % 4][:, WIDE - width:]
            h_all[j][c, mine[j]] = (gate * jax.nn.sigmoid(gate) * up).astype(jnp.bfloat16)
            launch(0, c, j, 4)

    def make_deltas(c, pair):
        streams = (pair, pair + 2)
        pair_arrived(1, c, pair)
        sums = {j: total_of(0, c, j) for j in streams}
        for j in streams:
            other = (j + 2) % 4
            width = SETS[j][1]
            gate = sums[j][:, :width]
            up = sums[other][:, WIDE - width:]
            grad = total_of(1, c, j)
            s = jax.nn.sigmoid(gate)
            d_all[c, j, mine[j], :, :width] = (grad * up * s * (1.0 + gate * (1.0 - s))).astype(jnp.bfloat16)
            d_all[c, other, mine[other], :, WIDE - width:] = (grad * gate * s).astype(jnp.bfloat16)
        for j in streams:
            launch(1, c, j, 4)

    def tokens(ref, c, j, lo, width, first=0, count=8):
        blocks = [ref[c, at(j, k // count, first + k % count), :, lo:lo + width] for k in range(2 * count)]
        return jnp.concatenate(blocks, axis=0)

    def hidden_of(c, j):
        return tokens(h_all[j], c, j, 0, SETS[j][1])

    def gate_delta_of(c, j, *some):
        return tokens(d_all.at[:, j], c, j, 0, SETS[j][1], *some)

    def up_delta_of(c, j, *some):
        other = (j + 2) % 4
        return tokens(d_all.at[:, other], c, other, WIDE - SETS[j][1], SETS[j][1], *some)

    def gathered(lane, c, ahead=False):
        def act(size, sem):
            remote(size, size, ssem.at[1], last_sem.at[sem], sibling).wait_recv()

        split = (lane, c) == (1, 2)
        if lane == 0:
            size = p_gu.at[c, 0]
        else:
            size = d_all.at[c, :, pl.ds(0, AHEAD if split else 8)]
        once(("doubled", lane, c), lambda: act(size, lane * CHUNKS + c))
        if split and not ahead:
            once("rest", lambda: act(d_all.at[c, :, pl.ds(0, 8 - AHEAD)], 2 * CHUNKS))

    def share_of(kind, c, first, count):
        rows = pl.ds(first * ROWS, count * ROWS)
        slot = c if first == 0 else 3
        return remote(
            o_part.at[kind, c, 1 - core, rows], o_sib.at[kind, c, rows],
            ss_sem.at[kind, slot], sr_sem.at[2 + kind, slot], sibling,
        )

    def scatter_start(kind, c, total, first=0, count=8):
        rows = count * ROWS
        o_part[kind, c, :, first * ROWS:first * ROWS + rows, :] = total.astype(jnp.bfloat16).reshape(2, rows, D)
        once(("sent", kind, c, first), lambda: gather_sent(kind, c if first == 0 else 3))
        share_of(kind, c, first, count).start()

    def scatter_along(kind, c, first=0, count=8):
        share_of(kind, c, first, count).wait_recv()
        lo, hi = first * ROWS, (first + count) * ROWS
        o_part[kind, c, core, lo:hi, :] = (
            o_part[kind, c, core, lo:hi, :].astype(jnp.float32) + o_sib[kind, c, lo:hi, :].astype(jnp.float32)
        ).astype(jnp.bfloat16)
        for d, row, rows, start in runs(c, first, count):
            if d != 0:
                remote(
                    o_part.at[kind, c, core, pl.ds(start, rows)],
                    o_z.at[kind, pl.ds(FAR.index(back(d)) * OWN + row, rows)],
                    zs_sem.at[kind, c], zr_sem.at[2 + kind, c], along[d],
                ).start()

    def landed(kind, c):
        whole = o_z.at[kind, pl.ds(0, HALF - (OWN if c == 0 else 0))]
        return remote(whole, whole, zs_sem.at[kind, c], zr_sem.at[2 + kind, c], sibling)

    def scatter_end(kind, c):
        landed(kind, c).wait_recv()
        for d, row, rows, start in runs(c):
            if d == 0:
                o_sum[kind] = o_part[kind, c, core, 0:OWN, :].astype(jnp.float32)
            else:
                spot = FAR.index(back(d)) * OWN + row
                o_sum[kind, row:row + rows, :] += o_z[kind, spot:spot + rows, :].astype(jnp.float32)
        if c == CHUNKS - 1:
            (out, ig)[kind][...] = o_sum[kind].astype(jnp.bfloat16)

    def output_part(c):
        gathered(0, c)
        total = None
        for j in range(4):
            lo, width = SETS[j]
            term = jnp.dot(hidden_of(c, j), wd[lo:lo + width, :], preferred_element_type=jnp.float32)
            total = term if total is None else total + term
        scatter_start(0, c, total)

    def input_grad_part(c):
        split = c >= CHUNKS - 1
        some = (((0, AHEAD), (AHEAD, 8 - AHEAD))[c - 2]) if split else (0, 8)
        gathered(1, min(c, 2), c == 2)
        total = None
        for j in range(4):
            lo, width = SETS[j]
            term = lax.dot_general(
                gate_delta_of(min(c, 2), j, *some), wg[:, lo:lo + width], contract_cols,
                preferred_element_type=jnp.float32,
            ) + lax.dot_general(
                up_delta_of(min(c, 2), j, *some), wu[:, lo:lo + width], contract_cols,
                preferred_element_type=jnp.float32,
            )
            total = term if total is None else total + term
        scatter_start(1, min(c, 2), total, *some)

    def along_part(kind, c):
        if kind == 1 and c >= CHUNKS - 1:
            scatter_along(1, 2, *((0, AHEAD), (AHEAD, 8 - AHEAD))[c - 2])
        else:
            scatter_along(kind, c)

    def over_tokens(left, right):
        a = jnp.concatenate([left(c) for c in range(CHUNKS)], axis=0)
        b = jnp.concatenate([right(c) for c in range(CHUNKS)], axis=0)
        return lax.dot_general(a, b, contract_rows, preferred_element_type=jnp.float32).astype(jnp.bfloat16)

    def down_grad(j):
        for c in range(CHUNKS):
            gathered(0, c)
        lo, width = SETS[j]
        dg[lo:lo + width, :] = over_tokens(lambda c: hidden_of(c, j), lambda c: rows_of(cts, c))

    def input_side_grads(j):
        for c in range(CHUNKS):
            gathered(1, c)
        lo, width = SETS[j]
        for res, of in ((gg, gate_delta_of), (ug, up_delta_of)):
            res[:, lo:lo + width] = over_tokens(lambda c: rows_of(xs, c), lambda c: of(c, j))

    def halve_or_double(lane, c, j, step):
        if step < 4:
            reduce_step(lane, c, j, step)
        else:
            arrived(lane, c, j, step - 1)
            launch(lane, c, j, step)

    acts = {
        "x": lambda c: gather_start(0, c), "c": lambda c: gather_start(1, c),
        "sx": lambda c: gather_share(0, c), "sc": lambda c: gather_share(1, c),
        "gu": gate_up, "hg": hidden_grad, "r": halve_or_double, "k": reduce_rest, "mh": make_hidden, "md": make_deltas,
        "m3": output_part, "m5": input_grad_part, "al": along_part, "ga": gate_up_early, "ha": hidden_grad_early, "en": scatter_end,
        "m4": down_grad, "m6": input_side_grads,
    }
    for act, *where in ORDER:
        acts[act](*where)

    left = [(r_gu, 0)]
    for j in range(4):
        left += [(h_all[j].at[:, pl.ds(0, BLOCKS - 1)], 1 + j), (r_hg[j], 5 + j)]
    left.append((d_all.at[:, :, pl.ds(0, BLOCKS - 1)], 9))
    for size, i in left:
        remote(size, size, ssem.at[i], last_sem.at[0], sibling).wait_send()
    gather_sent(0, 3)
    for kind in range(2):
        for c in range(CHUNKS):
            landed(kind, c).wait_send()
            if (kind, c) == (1, 2):
                share_of(1, 2, 0, AHEAD).wait_send()
                share_of(1, 2, AHEAD, 8 - AHEAD).wait_send()
            else:
                share_of(kind, c, 0, 8).wait_send()


def deliver(*refs):
    sources, results, sem = refs[:5], refs[5:10], refs[10]
    copies = []
    for src, dst in zip(sources, results):
        parts = 1 if src.shape[0] == OWN else PARTS
        step = src.shape[0] // parts
        for lo in range(0, src.shape[0], step):
            rows = pl.ds(lo, step)
            copies.append(pltpu.make_async_copy(src.at[rows], dst.at[rows], sem.at[len(copies)]))
    for copy in copies:
        copy.start()
    for copy in copies:
        copy.wait()


def local(inputs, w_gate, w_up, w_down, cotangent):
    bf16, f32 = jnp.bfloat16, jnp.float32
    vmem = pltpu.VMEM
    scratch = [
        vmem((OWN, D), bf16),
        vmem((OWN, D), bf16),
        vmem((2, CHUNKS * HALF, D), bf16),
        vmem((2, CHUNKS * HALF, D), bf16),
        vmem((D, F), bf16),
        vmem((D, F), bf16),
        vmem((F, D), bf16),
        vmem((CHUNKS, 4, BLOCKS, ROWS, WIDE), bf16),
        vmem((CHUNKS, 4, BLOCKS - 1, ROWS, WIDE), bf16),
        vmem((CHUNKS, 4, BLOCKS, ROWS, WIDE), bf16),
        vmem((2, CHUNKS, 2, HALF, D), bf16),
        vmem((2, CHUNKS, HALF, D), bf16),
        vmem((2, len(FAR) * OWN, D), bf16),
        vmem((2, OWN, D), f32),
    ]
    for count in (BLOCKS, BLOCKS - 1, BLOCKS):
        scratch += [vmem((CHUNKS, count, ROWS, width), bf16) for _, width in SETS]
    dma = pltpu.SemaphoreType.DMA
    scratch += [
        dma((5,)), dma((10,)), dma((2, CHUNKS, 4, 3)), dma((2, CHUNKS, 2)), dma((2 * CHUNKS + 1,)),
        dma((2, CHUNKS)), dma((4, CHUNKS)), dma((2, 4)), dma((4, 4)),
    ]
    whole = pl.BlockSpec(memory_space=pltpu.HBM)
    here = pl.BlockSpec(memory_space=pltpu.VMEM)
    results = (inputs, inputs, w_gate, w_up, w_down)
    held = pl.pallas_call(
        kernel,
        out_shape=tuple(pltpu.VMEM(a.shape, bf16) for a in results),
        in_specs=[whole] * 5,
        out_specs=[here] * 5,
        scratch_shapes=scratch,
        compiler_params=pltpu.CompilerParams(
            collective_id=0, has_side_effects=True, vmem_limit_bytes=40 * 2**20
        ),
    )(*[pltpu.with_memory_space_constraint(a, pltpu.HBM) for a in (inputs, w_gate, w_up, w_down, cotangent)])
    held = [pltpu.with_memory_space_constraint(a, pltpu.VMEM) for a in held]
    return pl.pallas_call(
        deliver,
        out_shape=tuple(jax.ShapeDtypeStruct(a.shape, bf16) for a in results),
        in_specs=[here] * 5,
        out_specs=[whole] * 5,
        scratch_shapes=[dma((2 + 3 * PARTS,))],
        compiler_params=pltpu.CompilerParams(vmem_limit_bytes=2**20),
    )(*held)


def solution(mesh):
    return jax.shard_map(
        local,
        mesh=mesh,
        in_specs=(P("col", "row"), P("row", "col"), P("row", "col"), P("col", "row"), P("col", "row")),
        out_specs=(P("col", "row"), P("col", "row"), P("row", "col"), P("row", "col"), P("col", "row")),
        check_vma=False,
    )
```
